32 devices in a mesh: gx: 8 (over z, x), gz: 4 (over y, core).
Axes of the slice: x: 2, y: 2, z: 4, core: 2. Of those that a mesh axis runs over, the one named last changes fastest.
Arguments:
- rhs_field: float32 [256, 32, 1024], P('gz', None, 'gx'), may hold values from -6 to 6
- heights: int32 [1024, 32], P('gx'), may hold values from 0 to 63
- vert_coef: float32 [256], replicated, may hold values from 30 to 300
- balance: int32 [8, 32], P('gx'), may hold values from 0 to 31, each once within a row
Outputs:
- pressure: float32 [256, 32, 1024], P('gz', None, 'gx')
- coarse_bundles: float32 [256, 4096], P('gx', 'gz')
The draws below stay inside these ranges and needn't reach their ends.
Inputs may be any that keep to these rules, and one draw needn't show every extreme that they name: `heights`: cells of a column below its height are inside a building. `balance`: each row lists every one of the 32 bundles of one source once.
All inputs are finite; a program needn't handle non-finite values.
Results may differ from the reference program's by a relative error of at most 0.0008.
Values sent between devices are 32-bit elements; how exact they have to be, the bound alone decides.
A program may use at most 128 MiB of HBM per device.

```python
import math
import jax
import jax.numpy as jnp
from jax import lax

NZ = 256
NY = 32
SWEEPS = 2
NX = 1024
OWNERS = 8
N_GX = 8


def with_ends(array, stream_key, smallest, high):
    dims = array.shape
    spot = [jax.random.randint(jax.random.fold_in(stream_key, axis), (), 0, dims[axis]) for axis in range(len(dims))]
    array = array.at[tuple(spot)].set(smallest)
    longest = dims.index(max(dims))
    spot[longest] = (spot[longest] + 1) % dims[longest]
    return array.at[tuple(spot)].set(high)


def levels(own_key, extent, shards, smallest, top_value):
    factor_of = 1.0
    for position, shards_of in shards:
        steps = jax.random.uniform(jax.random.fold_in(jax.random.fold_in(own_key, 6), position), (shards_of,), jnp.float32, smallest / len(shards), top_value / len(shards))
        factor_of = factor_of * jnp.repeat(jnp.exp(steps), extent[position] // shards_of).reshape((-1,) + (1,) * (len(extent) - 1 - position))
    return factor_of


def normal_values(own_key, dims, deviation, reach, split=(), kind=jnp.bfloat16):
    result = jax.random.normal(own_key, dims, jnp.float32) * deviation
    if len(split) > 0:
        result = levels(own_key, dims, split, -0.22, 0.18) * result
    return jnp.clip(result, min=-reach, max=reach).astype(kind)


def setup_inputs(seed: int = 0) -> dict:
    key_of = jax.random.split(jax.random.key(seed), 5)
    rhs_field = normal_values(key_of[0], (NZ, NY, NX), 1.0, 6.0, ((0, 4), (2, 8)), jnp.float32)
    heights = with_ends(jax.random.randint(key_of[1], (NX, NY), 0, NZ // 4), jax.random.fold_in(key_of[1], 1), 0, (NZ // 4) - 1).astype(jnp.int32)
    vert_coef = jnp.clip(jnp.exp(jax.random.uniform(key_of[2], (NZ,), jnp.float32, math.log(30.0), math.log(300.0))), 30.0, 300.0)
    balance = jax.vmap(lambda own: jax.random.permutation(own, NY))(jax.random.split(key_of[3], OWNERS)).reshape((OWNERS, NY)).astype(jnp.int32)
    return dict(rhs_field=rhs_field, heights=heights, vert_coef=vert_coef, balance=balance)


def line_bands(below_coef, above_coef, fluid_mask):
    below_full = below_coef[:, None, None] * fluid_mask
    above_full = above_coef[:, None, None] * fluid_mask
    centre = fluid_mask * (4.0 + below_coef[:, None, None] + above_coef[:, None, None]) + (1.0 - fluid_mask)
    return -below_full, centre, -above_full


def horizontal_sum(padded):
    return padded[:, 1:-1, :-2] + padded[:, 1:-1, 2:] + padded[:, :-2, 1:-1] + padded[:, 2:, 1:-1]


def thomas(lower_band, centre, upper_band, right_side):
    def forward(carry, items):
        prev_upper, prev_right = carry
        low_item, centre_item, up_item, right_item = items
        denom = centre_item - low_item * prev_upper
        new_upper = up_item / denom
        new_right = (right_item - low_item * prev_right) / denom
        return (new_upper, new_right), (new_upper, new_right)

    zeros_row = jnp.zeros_like(centre[0])
    _, (uppers, rights) = lax.scan(forward, (zeros_row, zeros_row), (lower_band, centre, upper_band, right_side))

    def backward(after, items):
        up_item, right_item = items
        value = right_item - up_item * after
        return value, value

    _, values = lax.scan(backward, zeros_row, (uppers, rights), reverse=True)
    return values


def solve_lines(right_side, fluid, below_coef, above_coef):
    block_width = math.gcd(NX, 512)
    block_count = NX // block_width

    def one_block(pair):
        right_part, fluid_part = pair
        lower_band, centre, upper_band = line_bands(below_coef, above_coef, fluid_part)
        return thomas(lower_band, centre, upper_band, right_part)

    stacked = (right_side.reshape(NZ, NY, block_count, block_width).transpose(2, 0, 1, 3),
               fluid.reshape(NZ, NY, block_count, block_width).transpose(2, 0, 1, 3))
    solved = lax.map(one_block, stacked)
    return solved.transpose(1, 2, 0, 3).reshape(NZ, NY, NX)


def reference(rhs_field, heights, vert_coef, balance):
    below_coef = vert_coef
    above_coef = jnp.concatenate([vert_coef[1:], jnp.zeros((1,), jnp.float32)])
    level_ids = jnp.arange(NZ, dtype=jnp.int32)
    fluid = (level_ids[:, None, None] >= heights.T[None]).astype(jnp.float32)
    parity_grid = (jnp.arange(NY, dtype=jnp.int32)[:, None] + jnp.arange(NX, dtype=jnp.int32)[None, :]) % 2
    pressure = jnp.zeros((NZ, NY, NX), jnp.float32)
    for sweep_step in range(SWEEPS):
        for colour in (0, 1):
            padded = jnp.pad(pressure, ((0, 0), (1, 1), (1, 1)))
            right_side = fluid * (rhs_field + horizontal_sum(padded))
            solved = solve_lines(right_side, fluid, below_coef, above_coef)
            pressure = jnp.where(parity_grid[None] == colour, solved, pressure)
    padded = jnp.pad(pressure, 1)
    applied = ((4.0 + below_coef[:, None, None] + above_coef[:, None, None]) * pressure
               - below_coef[:, None, None] * padded[:-2, 1:-1, 1:-1]
               - above_coef[:, None, None] * padded[2:, 1:-1, 1:-1]
               - horizontal_sum(padded[1:-1]))
    residual = fluid * (rhs_field - applied)
    coarse = residual.reshape(NZ // 2, 2, NY // 2, 2, NX // 2, 2).sum(axis=(1, 3, 5)) * 0.125
    blocks = coarse.reshape(NZ // 2, NY // 2, N_GX, 2, NX // (4 * N_GX)).transpose(2, 1, 3, 0, 4).reshape(N_GX, NY, -1)
    chosen = jnp.take_along_axis(blocks, balance[:, :, None], axis=1)
    per_owner = NY // N_GX
    coarse_bundles = chosen.reshape(N_GX, N_GX, per_owner, -1).transpose(1, 0, 2, 3).reshape(N_GX * NY, -1)
    return pressure, coarse_bundles
```

```python
import functools

import jax
import jax.numpy as jnp
from jax import lax
from jax.experimental import pallas as pl
from jax.experimental.pallas import tpu as pltpu
from jax.sharding import PartitionSpec as P

SWEEPS = 2
SOLVES = 2 * SWEEPS
UNROLL = 4
MESH = pl.DeviceIdType.MESH


def relax_kernel(
    n_gz,
    n_gx,
    rhs_ref,
    heights_ref,
    coef_ref,
    balance_ref,
    pool_ref,
    p_ref,
    out_ref,
    side_inv,
    low_inv,
    upper,
    low_spike,
    up_spike,
    local,
    delta,
    ends,
    spikes,
    reduced,
    firsts,
    lasts,
    halo_out,
    halo_in,
    pooled,
    bundles,
    outgoing,
    arrived,
    ends_send,
    ends_recv,
    spikes_send,
    spikes_recv,
    halo_send,
    halo_recv,
    tail_send,
    tail_recv,
):
    levels, rows, width = rhs_ref.shape
    total_z = coef_ref.shape[0]
    gz = lax.axis_index("gz")
    gx = lax.axis_index("gx")
    first_level = gz * levels

    barrier = pltpu.get_barrier_semaphore()
    for o in range(1, n_gz):
        pl.semaphore_signal(
            barrier, inc=1, device_id=(gx, lax.rem(gz + o, n_gz)), device_id_type=MESH
        )
    for o in range(1, n_gx):
        pl.semaphore_signal(
            barrier, inc=1, device_id=(lax.rem(gx + o, n_gx), gz), device_id_type=MESH
        )

    zero = jnp.zeros((rows, width), jnp.float32)
    one = jnp.ones((rows, width), jnp.float32)
    lane = lax.broadcasted_iota(jnp.int32, (rows, width), 1)
    row = lax.broadcasted_iota(jnp.int32, (rows, width), 0)
    parity = lax.rem(lane + row + gx * width, 2)
    at_left = lane == 0
    at_right = lane == width - 1
    at_top = row == 0
    at_bottom = row == rows - 1

    @pl.when(gx == 0)
    def _():
        for t in range(SOLVES):
            halo_in[t, 0] = zero

    @pl.when(gx == n_gx - 1)
    def _():
        for t in range(SOLVES):
            halo_in[t, 1] = zero

    def fluid_at(k):
        return (first_level + k >= heights_ref[...]).astype(jnp.float32)

    def factor(k, carry):
        up_before, d_before, spike_before = carry
        z = first_level + k
        below = coef_ref[z]
        above = jnp.where(z + 1 < total_z, coef_ref[jnp.minimum(z + 1, total_z - 1)], 0.0)
        fluid = fluid_at(k)
        low = -below * fluid
        centre = fluid * (4.0 + below + above) + (1.0 - fluid)
        inverse = 1.0 / (centre - low * up_before)
        up = -above * fluid * inverse
        low = low * inverse
        scale = fluid * inverse
        d = rhs_ref[k] * scale - low * d_before
        spike = -low * spike_before
        upper[k] = up
        low_inv[k] = low
        side_inv[k] = scale
        local[k] = d
        low_spike[k] = spike
        return up, d, spike

    def factor_back(i, carry):
        k = levels - 1 - i
        g_after, low_after, up_after = carry
        up = upper[k]
        g = local[k] - up * g_after
        low = low_spike[k] - up * low_after
        high = -up * up_after
        local[k] = g
        low_spike[k] = low
        up_spike[k] = high
        return g, low, high

    def around(cells, left_edge, right_edge):
        left = jnp.where(at_left, left_edge, pltpu.roll(cells, 1, 1))
        right = jnp.where(at_right, right_edge, pltpu.roll(cells, width - 1, 1))
        up = jnp.where(at_top, 0.0, pltpu.roll(cells, 1, 0))
        down = jnp.where(at_bottom, 0.0, pltpu.roll(cells, rows - 1, 0))
        return (left + right) + (up + down)

    def next_edge(edge):
        return pltpu.roll(edge, width - 1, 1)

    def forward(k, carry):
        d_before, left_edge, right_edge = carry
        side = rhs_ref[k] + around(p_ref[k], left_edge, right_edge)
        d = side * side_inv[k] - low_inv[k] * d_before
        local[k] = d
        return d, next_edge(left_edge), next_edge(right_edge)

    def backward(i, g_after):
        k = levels - 1 - i
        g = local[k] - upper[k] * g_after
        local[k] = g
        return g

    def halo_copies(t):
        to_right = pltpu.make_async_remote_copy(
            src_ref=halo_out.at[t, 0],
            dst_ref=halo_in.at[t, 0],
            send_sem=halo_send.at[t, 0],
            recv_sem=halo_recv.at[t, 0],
            device_id=(lax.rem(gx + 1, n_gx), gz),
            device_id_type=MESH,
        )
        to_left = pltpu.make_async_remote_copy(
            src_ref=halo_out.at[t, 1],
            dst_ref=halo_in.at[t, 1],
            send_sem=halo_send.at[t, 1],
            recv_sem=halo_recv.at[t, 1],
            device_id=(lax.rem(gx + n_gx - 1, n_gx), gz),
            device_id_type=MESH,
        )
        return to_right, to_left

    def start_halo(t):
        to_right, to_left = halo_copies(t)

        @pl.when(gx < n_gx - 1)
        def _():
            to_right.start()

        @pl.when(gx > 0)
        def _():
            to_left.start()

    def finish_halo(t):
        to_right, to_left = halo_copies(t)

        @pl.when(gx > 0)
        def _():
            to_left.wait_send()
            to_right.wait_recv()

        @pl.when(gx < n_gx - 1)
        def _():
            to_right.wait_send()
            to_left.wait_recv()

        left_edge = pltpu.roll(halo_in[t, 0], levels % width, 1)
        right_edge = pltpu.roll(halo_in[t, 1], (levels - 2) % width, 1)
        return left_edge, right_edge

    def column_copy(ref, send, recv, o):
        return pltpu.make_async_remote_copy(
            src_ref=ref.at[gz],
            dst_ref=ref.at[gz],
            send_sem=send.at[o - 1],
            recv_sem=recv.at[o - 1],
            device_id=(gx, lax.rem(gz + o, n_gz)),
            device_id_type=MESH,
        )

    for t in range(SOLVES):
        colour = t % 2
        if t == 0:
            lax.fori_loop(0, levels, factor, (zero, zero, one), unroll=UNROLL)
            d_last = local[levels - 1]
            g, low, high = lax.fori_loop(0, levels, factor_back, (zero, zero, one), unroll=UNROLL)
            spikes[gz, 0] = low
            spikes[gz, 1] = low_spike[levels - 1]
            spikes[gz, 2] = high
            spikes[gz, 3] = up_spike[levels - 1]
        else:
            left_edge, right_edge = finish_halo(t - 1)
            d_last, _, _ = lax.fori_loop(
                0, levels, forward, (zero, left_edge, right_edge), unroll=UNROLL
            )
            g = lax.fori_loop(0, levels, backward, zero, unroll=UNROLL)
        ends[t, gz, 0] = g
        ends[t, gz, 1] = d_last
        copies = [
            column_copy(ends.at[t], ends_send.at[t], ends_recv.at[t], o) for o in range(1, n_gz)
        ]
        if t == 0:
            copies += [column_copy(spikes, spikes_send, spikes_recv, o) for o in range(1, n_gz)]
            pl.semaphore_wait(barrier, n_gz + n_gx - 2)
        for copy in copies:
            copy.start()
        for copy in copies:
            copy.wait()

        if t == 0:
            beta = zero
            for s in range(n_gz):
                inverse = 1.0 / (1.0 - spikes[s, 0] * beta)
                reduced[s, 0] = beta
                reduced[s, 1] = inverse
                reduced[s, 2] = spikes[s, 2] * inverse
                beta = spikes[s, 3] + spikes[s, 1] * beta * reduced[s, 2]
                reduced[s, 3] = beta
        alpha = zero
        heads, tails = [], []
        for s in range(n_gz):
            head = (ends[t, s, 0] + spikes[s, 0] * alpha) * reduced[s, 1]
            alpha = ends[t, s, 1] + spikes[s, 1] * (alpha + reduced[s, 0] * head)
            heads.append(head)
            tails.append(alpha)
        after = zero
        firsts[n_gz] = zero
        lasts[0] = zero
        for s in reversed(range(n_gz)):
            lasts[s + 1] = tails[s] + reduced[s, 3] * after
            after = heads[s] + reduced[s, 2] * after
            firsts[s] = after
        below_value = lasts[gz]
        above_value = firsts[gz + 1]

        def correct(k, carry):
            to_right, to_left = carry
            value = local[k] + low_spike[k] * below_value + up_spike[k] * above_value
            before = zero if t == 0 else p_ref[k]
            cells = jnp.where(parity == colour, value, before)
            p_ref[k] = cells
            if t == SOLVES - 1:
                cells = cells - before
                delta[k] = cells
            to_right = jnp.where(at_right, cells, next_edge(to_right))
            to_left = jnp.where(at_left, cells, next_edge(to_left))
            return to_right, to_left

        to_right, to_left = lax.fori_loop(0, levels, correct, (zero, zero), unroll=UNROLL)
        halo_out[t, 0] = to_right
        halo_out[t, 1] = to_left
        start_halo(t)

    def coarsen(i, carry):
        left_edge, right_edge = carry
        total = zero
        for j in range(2):
            k = 2 * i + j
            total += fluid_at(k) * around(delta[k], left_edge, right_edge)
            left_edge, right_edge = next_edge(left_edge), next_edge(right_edge)
        local[i] = total
        return left_edge, right_edge

    lax.fori_loop(0, levels // 2, coarsen, finish_halo(SOLVES - 1), unroll=2)

    half = rows // 2
    per_row = width // (width // 4)
    chunks = levels // 2 // per_row
    for i in range(levels // 2):
        c, part = i // per_row, i % per_row
        pooled[c * half : (c + 1) * half, part * width : (part + 1) * width] = (
            local[i, pl.ds(0, half, 2), :] + local[i, pl.ds(1, half, 2), :]
        )
    packed = jnp.dot(
        pooled[...],
        pool_ref[...],
        preferred_element_type=jnp.float32,
        precision=lax.Precision.HIGHEST,
    )
    for c in range(chunks):
        for h in range(2):
            bundles[h * half : (h + 1) * half, c, :] = packed[
                c * half : (c + 1) * half, h * width : (h + 1) * width
            ]
    share = rows // n_gx
    for j in range(rows):
        b = balance_ref[0, j]
        outgoing[j] = bundles[(b & 1) * half + (b >> 1)]
    copies = []
    for o in range(1, n_gx):
        owner = lax.rem(gx + o, n_gx)
        copies.append(
            pltpu.make_async_remote_copy(
                src_ref=outgoing.at[pl.ds(owner * share, share)],
                dst_ref=arrived.at[pl.ds(gx * share, share)],
                send_sem=tail_send.at[o - 1],
                recv_sem=tail_recv.at[o - 1],
                device_id=(owner, gz),
                device_id_type=MESH,
            )
        )
    for copy in copies:
        copy.start()
    arrived[pl.ds(gx * share, share)] = outgoing[pl.ds(gx * share, share)]
    for copy in copies:
        copy.wait()
    for c in range(chunks):
        out_ref[:, c * width : (c + 1) * width] = arrived[:, c, :]


def on_device(n_gz, n_gx, rhs_field, heights, vert_coef, balance):
    levels, rows, width = rhs_field.shape
    per_row = 4
    chunks = levels // 2 // per_row
    spot = jnp.arange(per_row * width, dtype=jnp.int32)[:, None]
    target = jnp.arange(2 * width, dtype=jnp.int32)[None, :]
    quarter = width // 4
    coarse_x = (spot % width) // 2
    pool = jnp.where(
        (target // width == coarse_x // quarter)
        & (target % width == (spot // width) * quarter + coarse_x % quarter),
        0.125,
        0.0,
    ).astype(jnp.float32)
    vmem = pl.BlockSpec(memory_space=pltpu.VMEM)
    smem = pl.BlockSpec(memory_space=pltpu.SMEM)
    slab = pltpu.VMEM((levels, rows, width), jnp.float32)
    plane = (rows, width)

    def planes(*lead):
        return pltpu.VMEM(lead + plane, jnp.float32)

    def sems(*lead):
        return pltpu.SemaphoreType.DMA(lead)

    pressure, coarse = pl.pallas_call(
        functools.partial(relax_kernel, n_gz, n_gx),
        out_shape=(
            jax.ShapeDtypeStruct(rhs_field.shape, jnp.float32),
            jax.ShapeDtypeStruct((rows, chunks * width), jnp.float32),
        ),
        in_specs=[vmem, vmem, smem, smem, vmem],
        out_specs=(vmem, vmem),
        scratch_shapes=[slab] * 7
        + [
            planes(SOLVES, n_gz, 2),
            planes(n_gz, 4),
            planes(n_gz, 4),
            planes(n_gz + 1),
            planes(n_gz + 1),
            planes(SOLVES, 2),
            planes(SOLVES, 2),
            pltpu.VMEM((chunks * rows // 2, per_row * width), jnp.float32),
            pltpu.VMEM((rows, chunks, width), jnp.float32),
            pltpu.VMEM((rows, chunks, width), jnp.float32),
            pltpu.VMEM((rows, chunks, width), jnp.float32),
            sems(SOLVES, n_gz - 1),
            sems(SOLVES, n_gz - 1),
            sems(n_gz - 1),
            sems(n_gz - 1),
            sems(SOLVES, 2),
            sems(SOLVES, 2),
            sems(n_gx - 1),
            sems(n_gx - 1),
        ],
        compiler_params=pltpu.CompilerParams(
            collective_id=0, has_side_effects=True, vmem_limit_bytes=32 * 1024 * 1024
        ),
    )(rhs_field, heights.T, vert_coef, balance, pool)
    return pressure, coarse


def solution(mesh):
    placed = (P("gz", None, "gx"), P("gx", None), P(), P("gx", None))
    return jax.shard_map(
        functools.partial(on_device, mesh.shape["gz"], mesh.shape["gx"]),
        mesh=mesh,
        in_specs=placed,
        out_specs=(P("gz", None, "gx"), P("gx", "gz")),
        check_vma=False,
    )
```

```python
import functools

import jax
import jax.numpy as jnp
from jax import lax
from jax.experimental import pallas as pl
from jax.experimental.pallas import tpu as pltpu
from jax.sharding import PartitionSpec as P

SWEEPS = 2
SOLVES = 2 * SWEEPS
UNROLL = 8
MESH = pl.DeviceIdType.MESH


def relax_kernel(
    n_gz,
    n_gx,
    rhs_ref,
    heights_ref,
    coef_ref,
    balance_ref,
    pool_ref,
    p_ref,
    out_ref,
    side_inv,
    low_inv,
    upper,
    low_spike,
    up_spike,
    local,
    delta,
    ends,
    spikes,
    reduced,
    firsts,
    lasts,
    halo_out,
    halo_in,
    pooled,
    bundles,
    outgoing,
    arrived,
    ends_send,
    ends_recv,
    spikes_send,
    spikes_recv,
    halo_send,
    halo_recv,
    tail_send,
    tail_recv,
):
    levels, rows, width = rhs_ref.shape
    total_z = coef_ref.shape[0]
    gz = lax.axis_index("gz")
    gx = lax.axis_index("gx")
    first_level = gz * levels

    barrier = pltpu.get_barrier_semaphore()
    for o in range(1, n_gz):
        pl.semaphore_signal(
            barrier, inc=1, device_id=(gx, lax.rem(gz + o, n_gz)), device_id_type=MESH
        )
    for o in range(1, n_gx):
        pl.semaphore_signal(
            barrier, inc=1, device_id=(lax.rem(gx + o, n_gx), gz), device_id_type=MESH
        )

    zero = jnp.zeros((rows, width), jnp.float32)
    one = jnp.ones((rows, width), jnp.float32)
    lane = lax.broadcasted_iota(jnp.int32, (rows, width), 1)
    row = lax.broadcasted_iota(jnp.int32, (rows, width), 0)
    parity = lax.rem(lane + row + gx * width, 2)
    at_left = lane == 0
    at_right = lane == width - 1
    at_top = row == 0
    at_bottom = row == rows - 1

    @pl.when(gx == 0)
    def _():
        for t in range(SOLVES):
            halo_in[t, 0] = zero

    @pl.when(gx == n_gx - 1)
    def _():
        for t in range(SOLVES):
            halo_in[t, 1] = zero

    def fluid_at(k):
        return (first_level + k >= heights_ref[...]).astype(jnp.float32)

    def factor(k, carry):
        up_before, d_before, spike_before = carry
        z = first_level + k
        below = coef_ref[z]
        above = jnp.where(z + 1 < total_z, coef_ref[jnp.minimum(z + 1, total_z - 1)], 0.0)
        fluid = fluid_at(k)
        low = -below * fluid
        centre = fluid * (4.0 + below + above) + (1.0 - fluid)
        inverse = 1.0 / (centre - low * up_before)
        up = -above * fluid * inverse
        low = low * inverse
        scale = fluid * inverse
        d = rhs_ref[k] * scale - low * d_before
        spike = -low * spike_before
        upper[k] = up
        low_inv[k] = low
        side_inv[k] = scale
        local[k] = d
        low_spike[k] = spike
        return up, d, spike

    def factor_back(i, carry):
        k = levels - 1 - i
        g_after, low_after, up_after = carry
        up = upper[k]
        g = local[k] - up * g_after
        low = low_spike[k] - up * low_after
        high = -up * up_after
        local[k] = g
        low_spike[k] = low
        up_spike[k] = high
        return g, low, high

    def turned(cells, shift):
        shift = shift % width
        return cells if shift == 0 else pltpu.roll(cells, shift, 1)

    def around(cells, edge, edge_mask):
        left = jnp.where(at_left, 0.0, pltpu.roll(cells, 1, 1))
        right = jnp.where(at_right, 0.0, pltpu.roll(cells, width - 1, 1))
        up = jnp.where(at_top, 0.0, pltpu.roll(cells, 1, 0))
        down = jnp.where(at_bottom, 0.0, pltpu.roll(cells, rows - 1, 0))
        return (left + right) + (up + down) + jnp.where(edge_mask, edge, 0.0)

    def forward(edge_mask, step, carry):
        d, edges = carry
        for j in range(UNROLL):
            k = step * UNROLL + j
            side = rhs_ref[k] + around(p_ref[k], turned(edges, -j), edge_mask)
            d = side * side_inv[k] - low_inv[k] * d
            local[k] = d
        return d, turned(edges, -UNROLL)

    def backward(i, g_after):
        k = levels - 1 - i
        g = local[k] - upper[k] * g_after
        local[k] = g
        return g

    def halo_copies(t):
        to_right = pltpu.make_async_remote_copy(
            src_ref=halo_out.at[t, 0],
            dst_ref=halo_in.at[t, 0],
            send_sem=halo_send.at[t, 0],
            recv_sem=halo_recv.at[t, 0],
            device_id=(lax.rem(gx + 1, n_gx), gz),
            device_id_type=MESH,
        )
        to_left = pltpu.make_async_remote_copy(
            src_ref=halo_out.at[t, 1],
            dst_ref=halo_in.at[t, 1],
            send_sem=halo_send.at[t, 1],
            recv_sem=halo_recv.at[t, 1],
            device_id=(lax.rem(gx + n_gx - 1, n_gx), gz),
            device_id_type=MESH,
        )
        return to_right, to_left

    def start_halo(t):
        to_right, to_left = halo_copies(t)

        @pl.when(gx < n_gx - 1)
        def _():
            to_right.start()

        @pl.when(gx > 0)
        def _():
            to_left.start()

    def finish_halo(t, colour):
        to_right, to_left = halo_copies(t)

        @pl.when(gx > 0)
        def _():
            to_left.wait_send()
            to_right.wait_recv()

        @pl.when(gx < n_gx - 1)
        def _():
            to_right.wait_send()
            to_left.wait_recv()

        left_edge = pltpu.roll(halo_in[t, 0], levels % width, 1)
        right_edge = pltpu.roll(halo_in[t, 1], (levels - 2) % width, 1)
        needs_left = lax.rem(row + gx * width, 2) == colour
        return jnp.where(needs_left, left_edge, right_edge)

    def column_copy(ref, send, recv, o):
        return pltpu.make_async_remote_copy(
            src_ref=ref.at[gz],
            dst_ref=ref.at[gz],
            send_sem=send.at[o - 1],
            recv_sem=recv.at[o - 1],
            device_id=(gx, lax.rem(gz + o, n_gz)),
            device_id_type=MESH,
        )

    for t in range(SOLVES):
        colour = t % 2
        if t == 0:
            lax.fori_loop(0, levels, factor, (zero, zero, one), unroll=UNROLL)
            d_last = local[levels - 1]
            g, low, high = lax.fori_loop(0, levels, factor_back, (zero, zero, one), unroll=UNROLL)
            spikes[gz, 0] = low
            spikes[gz, 1] = low_spike[levels - 1]
            spikes[gz, 2] = high
            spikes[gz, 3] = up_spike[levels - 1]
        else:
            edge_mask = (at_left | at_right) & (parity == colour)
            d_last, _ = lax.fori_loop(
                0,
                levels // UNROLL,
                functools.partial(forward, edge_mask),
                (zero, finish_halo(t - 1, colour)),
            )
            g = lax.fori_loop(0, levels, backward, zero, unroll=UNROLL)
        ends[t, gz, 0] = g
        ends[t, gz, 1] = d_last
        copies = [
            column_copy(ends.at[t], ends_send.at[t], ends_recv.at[t], o) for o in range(1, n_gz)
        ]
        if t == 0:
            copies += [column_copy(spikes, spikes_send, spikes_recv, o) for o in range(1, n_gz)]
            pl.semaphore_wait(barrier, n_gz + n_gx - 2)
        for copy in copies:
            copy.start()
        for copy in copies:
            copy.wait()

        if t == 0:
            beta = zero
            for s in range(n_gz):
                inverse = 1.0 / (1.0 - spikes[s, 0] * beta)
                reduced[s, 0] = beta
                reduced[s, 1] = inverse
                reduced[s, 2] = spikes[s, 2] * inverse
                beta = spikes[s, 3] + spikes[s, 1] * beta * reduced[s, 2]
                reduced[s, 3] = beta
        alpha = zero
        heads, tails = [], []
        for s in range(n_gz):
            head = (ends[t, s, 0] + spikes[s, 0] * alpha) * reduced[s, 1]
            alpha = ends[t, s, 1] + spikes[s, 1] * (alpha + reduced[s, 0] * head)
            heads.append(head)
            tails.append(alpha)
        after = zero
        firsts[n_gz] = zero
        lasts[0] = zero
        for s in reversed(range(n_gz)):
            lasts[s + 1] = tails[s] + reduced[s, 3] * after
            after = heads[s] + reduced[s, 2] * after
            firsts[s] = after
        below_value = lasts[gz]
        above_value = firsts[gz + 1]

        def correct(step, carry):
            to_right, to_left = (turned(edge, -UNROLL) for edge in carry)
            for j in range(UNROLL):
                k = step * UNROLL + j
                value = local[k] + low_spike[k] * below_value + up_spike[k] * above_value
                before = zero if t == 0 else p_ref[k]
                cells = jnp.where(parity == colour, value, before)
                p_ref[k] = cells
                if t == SOLVES - 1:
                    cells = cells - before
                    delta[k] = cells
                moved = turned(cells, 1 + j - UNROLL)
                to_right = jnp.where(lane == width - UNROLL + j, moved, to_right)
                to_left = jnp.where(lane == (width + 1 - UNROLL + j) % width, moved, to_left)
            return to_right, to_left

        to_right, to_left = lax.fori_loop(0, levels // UNROLL, correct, (zero, zero))
        halo_out[t, 0] = to_right
        halo_out[t, 1] = to_left
        start_halo(t)

    edge_mask = (at_left | at_right) & (parity == 0)

    def coarsen(step, edges):
        for j in range(0, UNROLL, 2):
            k = step * UNROLL + j
            local[step * (UNROLL // 2) + j // 2] = fluid_at(k) * around(
                delta[k], turned(edges, -j), edge_mask
            ) + fluid_at(k + 1) * around(delta[k + 1], turned(edges, -j - 1), edge_mask)
        return turned(edges, -UNROLL)

    lax.fori_loop(0, levels // UNROLL, coarsen, finish_halo(SOLVES - 1, 0))

    half = rows // 2
    per_row = width // (width // 4)
    chunks = levels // 2 // per_row
    for i in range(levels // 2):
        c, part = i // per_row, i % per_row
        pooled[c * half : (c + 1) * half, part * width : (part + 1) * width] = (
            local[i, pl.ds(0, half, 2), :] + local[i, pl.ds(1, half, 2), :]
        )
    packed = jnp.dot(
        pooled[...],
        pool_ref[...],
        preferred_element_type=jnp.float32,
        precision=lax.Precision.HIGHEST,
    )
    for c in range(chunks):
        for h in range(2):
            bundles[h * half : (h + 1) * half, c, :] = packed[
                c * half : (c + 1) * half, h * width : (h + 1) * width
            ]
    share = rows // n_gx
    for j in range(rows):
        b = balance_ref[0, j]
        outgoing[j] = bundles[(b & 1) * half + (b >> 1)]
    copies = []
    for o in range(1, n_gx):
        owner = lax.rem(gx + o, n_gx)
        copies.append(
            pltpu.make_async_remote_copy(
                src_ref=outgoing.at[pl.ds(owner * share, share)],
                dst_ref=arrived.at[pl.ds(gx * share, share)],
                send_sem=tail_send.at[o - 1],
                recv_sem=tail_recv.at[o - 1],
                device_id=(owner, gz),
                device_id_type=MESH,
            )
        )
    for copy in copies:
        copy.start()
    arrived[pl.ds(gx * share, share)] = outgoing[pl.ds(gx * share, share)]
    for copy in copies:
        copy.wait()
    for c in range(chunks):
        out_ref[:, c * width : (c + 1) * width] = arrived[:, c, :]


def on_device(n_gz, n_gx, rhs_field, heights, vert_coef, balance):
    levels, rows, width = rhs_field.shape
    per_row = 4
    chunks = levels // 2 // per_row
    spot = jnp.arange(per_row * width, dtype=jnp.int32)[:, None]
    target = jnp.arange(2 * width, dtype=jnp.int32)[None, :]
    quarter = width // 4
    coarse_x = (spot % width) // 2
    pool = jnp.where(
        (target // width == coarse_x // quarter)
        & (target % width == (spot // width) * quarter + coarse_x % quarter),
        0.125,
        0.0,
    ).astype(jnp.float32)
    vmem = pl.BlockSpec(memory_space=pltpu.VMEM)
    smem = pl.BlockSpec(memory_space=pltpu.SMEM)
    slab = pltpu.VMEM((levels, rows, width), jnp.float32)
    plane = (rows, width)

    def planes(*lead):
        return pltpu.VMEM(lead + plane, jnp.float32)

    def sems(*lead):
        return pltpu.SemaphoreType.DMA(lead)

    pressure, coarse = pl.pallas_call(
        functools.partial(relax_kernel, n_gz, n_gx),
        out_shape=(
            jax.ShapeDtypeStruct(rhs_field.shape, jnp.float32),
            jax.ShapeDtypeStruct((rows, chunks * width), jnp.float32),
        ),
        in_specs=[vmem, vmem, smem, smem, vmem],
        out_specs=(vmem, vmem),
        scratch_shapes=[slab] * 7
        + [
            planes(SOLVES, n_gz, 2),
            planes(n_gz, 4),
            planes(n_gz, 4),
            planes(n_gz + 1),
            planes(n_gz + 1),
            planes(SOLVES, 2),
            planes(SOLVES, 2),
            pltpu.VMEM((chunks * rows // 2, per_row * width), jnp.float32),
            pltpu.VMEM((rows, chunks, width), jnp.float32),
            pltpu.VMEM((rows, chunks, width), jnp.float32),
            pltpu.VMEM((rows, chunks, width), jnp.float32),
            sems(SOLVES, n_gz - 1),
            sems(SOLVES, n_gz - 1),
            sems(n_gz - 1),
            sems(n_gz - 1),
            sems(SOLVES, 2),
            sems(SOLVES, 2),
            sems(n_gx - 1),
            sems(n_gx - 1),
        ],
        compiler_params=pltpu.CompilerParams(
            collective_id=0, has_side_effects=True, vmem_limit_bytes=32 * 1024 * 1024
        ),
    )(rhs_field, heights.T, vert_coef, balance, pool)
    return pressure, coarse


def solution(mesh):
    placed = (P("gz", None, "gx"), P("gx", None), P(), P("gx", None))
    return jax.shard_map(
        functools.partial(on_device, mesh.shape["gz"], mesh.shape["gx"]),
        mesh=mesh,
        in_specs=placed,
        out_specs=(P("gz", None, "gx"), P("gx", "gz")),
        check_vma=False,
    )
```

```python
import functools

import jax
import jax.numpy as jnp
from jax import lax
from jax.experimental import pallas as pl
from jax.experimental.pallas import tpu as pltpu
from jax.sharding import PartitionSpec as P

SWEEPS = 2
SOLVES = 2 * SWEEPS
UNROLL = 8
MESH = pl.DeviceIdType.MESH


def relax_kernel(
    n_gz,
    n_gx,
    rhs_ref,
    heights_ref,
    coef_ref,
    balance_ref,
    pool_ref,
    p_ref,
    out_ref,
    side_inv,
    low_inv,
    upper,
    low_spike,
    up_spike,
    local,
    delta,
    ends,
    spikes,
    reduced,
    firsts,
    lasts,
    edge_spikes,
    halo_out,
    halo_in,
    pooled,
    bundles,
    outgoing,
    arrived,
    ends_send,
    ends_recv,
    spikes_send,
    spikes_recv,
    halo_send,
    halo_recv,
    tail_send,
    tail_recv,
):
    levels, rows, width = rhs_ref.shape
    total_z = coef_ref.shape[0]
    gz = lax.axis_index("gz")
    gx = lax.axis_index("gx")
    first_level = gz * levels

    barrier = pltpu.get_barrier_semaphore()
    for o in range(1, n_gz):
        pl.semaphore_signal(
            barrier, inc=1, device_id=(gx, lax.rem(gz + o, n_gz)), device_id_type=MESH
        )
    for o in range(1, n_gx):
        pl.semaphore_signal(
            barrier, inc=1, device_id=(lax.rem(gx + o, n_gx), gz), device_id_type=MESH
        )

    zero = jnp.zeros((rows, width), jnp.float32)
    one = jnp.ones((rows, width), jnp.float32)
    lane = lax.broadcasted_iota(jnp.int32, (rows, width), 1)
    row = lax.broadcasted_iota(jnp.int32, (rows, width), 0)
    parity = lax.rem(lane + row + gx * width, 2)
    at_left = lane == 0
    at_right = lane == width - 1
    at_top = row == 0
    at_bottom = row == rows - 1

    @pl.when(gx == 0)
    def _():
        for t in range(SOLVES):
            halo_in[t, 0] = zero

    @pl.when(gx == n_gx - 1)
    def _():
        for t in range(SOLVES):
            halo_in[t, 1] = zero

    def fluid_at(k):
        return (first_level + k >= heights_ref[...]).astype(jnp.float32)

    def factor(k, carry):
        up_before, d_before, spike_before = carry
        z = first_level + k
        below = coef_ref[z]
        above = jnp.where(z + 1 < total_z, coef_ref[jnp.minimum(z + 1, total_z - 1)], 0.0)
        fluid = fluid_at(k)
        low = -below * fluid
        centre = fluid * (4.0 + below + above) + (1.0 - fluid)
        inverse = 1.0 / (centre - low * up_before)
        up = -above * fluid * inverse
        low = low * inverse
        scale = fluid * inverse
        d = rhs_ref[k] * scale - low * d_before
        spike = -low * spike_before
        upper[k] = up
        low_inv[k] = low
        side_inv[k] = scale
        local[k] = d
        low_spike[k] = spike
        return up, d, spike

    def turned(cells, shift):
        shift = shift % width
        return cells if shift == 0 else pltpu.roll(cells, shift, 1)

    def around(cells, edge, edge_mask):
        left = jnp.where(at_left, 0.0, pltpu.roll(cells, 1, 1))
        right = jnp.where(at_right, 0.0, pltpu.roll(cells, width - 1, 1))
        up = jnp.where(at_top, 0.0, pltpu.roll(cells, 1, 0))
        down = jnp.where(at_bottom, 0.0, pltpu.roll(cells, rows - 1, 0))
        return (left + right) + (up + down) + jnp.where(edge_mask, edge, 0.0)

    def forward(edge_mask, step, carry):
        d, edges = carry
        for j in range(UNROLL):
            k = step * UNROLL + j
            side = rhs_ref[k] + around(p_ref[k], turned(edges, -j), edge_mask)
            d = side * side_inv[k] - low_inv[k] * d
            local[k] = d
        return d, turned(edges, -UNROLL)

    def with_edge(packed, cells, i, offset):
        return jnp.where(lane == i + offset, turned(cells, i + 1), packed)

    def factor_back(step, carry):
        g, low, high, g_edge, low_right, low_left, high_right, high_left = carry
        base = levels - UNROLL * (step + 1)
        g_edge, low_right, low_left, high_right, high_left = (
            turned(edge, UNROLL)
            for edge in (g_edge, low_right, low_left, high_right, high_left)
        )
        for i in reversed(range(UNROLL)):
            k = base + i
            up = upper[k]
            g = local[k] - up * g
            low = low_spike[k] - up * low
            high = -up * high
            local[k] = g
            low_spike[k] = low
            up_spike[k] = high
            g_edge = with_edge(g_edge, g, i, edge_lane(0))
            low_right = with_edge(low_right, low, i, 0)
            low_left = with_edge(low_left, low, i, 1)
            high_right = with_edge(high_right, high, i, 0)
            high_left = with_edge(high_left, high, i, 1)
        return g, low, high, g_edge, low_right, low_left, high_right, high_left

    def backward(offset, step, carry):
        g, g_edge = carry
        base = levels - UNROLL * (step + 1)
        g_edge = turned(g_edge, UNROLL)
        for i in reversed(range(UNROLL)):
            k = base + i
            g = local[k] - upper[k] * g
            local[k] = g
            g_edge = with_edge(g_edge, g, i, offset)
        return g, g_edge

    def from_left(colour):
        return lax.rem(row + gx * width, 2) == colour

    def edge_lane(colour):
        return jnp.where(from_left(colour), 1, 0)

    def halo_copies(t):
        to_right = pltpu.make_async_remote_copy(
            src_ref=halo_out.at[t],
            dst_ref=halo_in.at[t, 0],
            send_sem=halo_send.at[t, 0],
            recv_sem=halo_recv.at[t, 0],
            device_id=(lax.rem(gx + 1, n_gx), gz),
            device_id_type=MESH,
        )
        to_left = pltpu.make_async_remote_copy(
            src_ref=halo_out.at[t],
            dst_ref=halo_in.at[t, 1],
            send_sem=halo_send.at[t, 1],
            recv_sem=halo_recv.at[t, 1],
            device_id=(lax.rem(gx + n_gx - 1, n_gx), gz),
            device_id_type=MESH,
        )
        return to_right, to_left

    def start_halo(t):
        to_right, to_left = halo_copies(t)

        @pl.when(gx < n_gx - 1)
        def _():
            to_right.start()

        @pl.when(gx > 0)
        def _():
            to_left.start()

    def finish_halo(t, colour):
        to_right, to_left = halo_copies(t)

        @pl.when(gx > 0)
        def _():
            to_left.wait_send()
            to_right.wait_recv()

        @pl.when(gx < n_gx - 1)
        def _():
            to_right.wait_send()
            to_left.wait_recv()

        left_edge = halo_in[t, 0]
        right_edge = turned(halo_in[t, 1], -2)
        return jnp.where(from_left(colour), left_edge, right_edge)

    def column_copy(ref, send, recv, o):
        return pltpu.make_async_remote_copy(
            src_ref=ref,
            dst_ref=ref,
            send_sem=send.at[o - 1],
            recv_sem=recv.at[o - 1],
            device_id=(gx, lax.rem(gz + o, n_gz)),
            device_id_type=MESH,
        )

    for t in range(SOLVES):
        colour = t % 2
        if t == 0:
            lax.fori_loop(0, levels, factor, (zero, zero, one), unroll=UNROLL)
            d_last = local[levels - 1]
            spikes[gz, 0] = low_spike[levels - 1]
            spikes[gz, 1] = -upper[levels - 1]
            pl.semaphore_wait(barrier, n_gz + n_gx - 2)
            early = [
                column_copy(
                    spikes.at[gz, pl.ds(0, 2)], spikes_send.at[0], spikes_recv.at[0], o
                )
                for o in range(1, n_gz)
            ]
            for copy in early:
                copy.start()
            g, low, high, g_edge, *spike_edges = lax.fori_loop(
                0, levels // UNROLL, factor_back, (zero, zero, one) + (zero,) * 5
            )
            spikes[gz, 2] = low
            spikes[gz, 3] = high
            for e in range(4):
                edge_spikes[e] = spike_edges[e]
        else:
            edge_mask = (at_left | at_right) & (parity == colour)
            d_last, _ = lax.fori_loop(
                0,
                levels // UNROLL,
                functools.partial(forward, edge_mask),
                (zero, finish_halo(t - 1, colour)),
            )
            g, g_edge = lax.fori_loop(
                0,
                levels // UNROLL,
                functools.partial(backward, edge_lane(colour)),
                (zero, zero),
            )
        ends[t, gz, 0] = g
        ends[t, gz, 1] = d_last
        copies = [
            column_copy(ends.at[t, gz], ends_send.at[t], ends_recv.at[t], o)
            for o in range(1, n_gz)
        ]
        if t == 0:
            copies += [
                column_copy(
                    spikes.at[gz, pl.ds(2, 2)], spikes_send.at[1], spikes_recv.at[1], o
                )
                for o in range(1, n_gz)
            ]
        for copy in copies:
            copy.start()
        if t == 0:
            copies += early
        for copy in copies:
            copy.wait()

        if t == 0:
            beta = zero
            for s in range(n_gz):
                inverse = 1.0 / (1.0 - spikes[s, 2] * beta)
                reduced[s, 0] = beta
                reduced[s, 1] = inverse
                reduced[s, 2] = spikes[s, 3] * inverse
                beta = spikes[s, 1] + spikes[s, 0] * beta * reduced[s, 2]
                reduced[s, 3] = beta
        alpha = zero
        heads, tails = [], []
        for s in range(n_gz):
            head = (ends[t, s, 0] + spikes[s, 2] * alpha) * reduced[s, 1]
            alpha = ends[t, s, 1] + spikes[s, 0] * (alpha + reduced[s, 0] * head)
            heads.append(head)
            tails.append(alpha)
        after = zero
        firsts[n_gz] = zero
        lasts[0] = zero
        for s in reversed(range(n_gz)):
            lasts[s + 1] = tails[s] + reduced[s, 3] * after
            after = heads[s] + reduced[s, 2] * after
            firsts[s] = after
        below_value = lasts[gz]
        above_value = firsts[gz + 1]

        sent = from_left(colour)
        below_edge = jnp.where(sent, below_value[:, :1], below_value[:, width - 1 :])
        above_edge = jnp.where(sent, above_value[:, :1], above_value[:, width - 1 :])
        low_edge = jnp.where(sent, edge_spikes[1], edge_spikes[0])
        high_edge = jnp.where(sent, edge_spikes[3], edge_spikes[2])
        edge_cells = g_edge + low_edge * below_edge + high_edge * above_edge
        if t == SOLVES - 1:
            edge_cells = edge_cells - halo_out[t - 2]
        halo_out[t] = edge_cells
        start_halo(t)

        def correct(k, carry):
            value = local[k] + low_spike[k] * below_value + up_spike[k] * above_value
            before = zero if t == 0 else p_ref[k]
            cells = jnp.where(parity == colour, value, before)
            p_ref[k] = cells
            if t == SOLVES - 1:
                delta[k] = cells - before
            return carry

        lax.fori_loop(0, levels, correct, 0, unroll=UNROLL)

    edge_mask = (at_left | at_right) & (parity == 0)

    def coarsen(step, edges):
        for j in range(0, UNROLL, 2):
            k = step * UNROLL + j
            local[step * (UNROLL // 2) + j // 2] = fluid_at(k) * around(
                delta[k], turned(edges, -j), edge_mask
            ) + fluid_at(k + 1) * around(delta[k + 1], turned(edges, -j - 1), edge_mask)
        return turned(edges, -UNROLL)

    lax.fori_loop(0, levels // UNROLL, coarsen, finish_halo(SOLVES - 1, 0))

    half = rows // 2
    per_row = width // (width // 4)
    chunks = levels // 2 // per_row
    for i in range(levels // 2):
        c, part = i // per_row, i % per_row
        pooled[c * half : (c + 1) * half, part * width : (part + 1) * width] = (
            local[i, pl.ds(0, half, 2), :] + local[i, pl.ds(1, half, 2), :]
        )
    packed = jnp.dot(
        pooled[...],
        pool_ref[...],
        preferred_element_type=jnp.float32,
        precision=lax.Precision.HIGHEST,
    )
    for c in range(chunks):
        for h in range(2):
            bundles[h * half : (h + 1) * half, c, :] = packed[
                c * half : (c + 1) * half, h * width : (h + 1) * width
            ]
    share = rows // n_gx
    for j in range(rows):
        b = balance_ref[0, j]
        outgoing[j] = bundles[(b & 1) * half + (b >> 1)]
    copies = []
    for o in range(1, n_gx):
        owner = lax.rem(gx + o, n_gx)
        copies.append(
            pltpu.make_async_remote_copy(
                src_ref=outgoing.at[pl.ds(owner * share, share)],
                dst_ref=arrived.at[pl.ds(gx * share, share)],
                send_sem=tail_send.at[o - 1],
                recv_sem=tail_recv.at[o - 1],
                device_id=(owner, gz),
                device_id_type=MESH,
            )
        )
    for copy in copies:
        copy.start()
    arrived[pl.ds(gx * share, share)] = outgoing[pl.ds(gx * share, share)]
    for copy in copies:
        copy.wait()
    for c in range(chunks):
        out_ref[:, c * width : (c + 1) * width] = arrived[:, c, :]


def on_device(n_gz, n_gx, rhs_field, heights, vert_coef, balance):
    levels, rows, width = rhs_field.shape
    per_row = 4
    chunks = levels // 2 // per_row
    spot = jnp.arange(per_row * width, dtype=jnp.int32)[:, None]
    target = jnp.arange(2 * width, dtype=jnp.int32)[None, :]
    quarter = width // 4
    coarse_x = (spot % width) // 2
    pool = jnp.where(
        (target // width == coarse_x // quarter)
        & (target % width == (spot // width) * quarter + coarse_x % quarter),
        0.125,
        0.0,
    ).astype(jnp.float32)
    vmem = pl.BlockSpec(memory_space=pltpu.VMEM)
    smem = pl.BlockSpec(memory_space=pltpu.SMEM)
    slab = pltpu.VMEM((levels, rows, width), jnp.float32)
    plane = (rows, width)

    def planes(*lead):
        return pltpu.VMEM(lead + plane, jnp.float32)

    def sems(*lead):
        return pltpu.SemaphoreType.DMA(lead)

    pressure, coarse = pl.pallas_call(
        functools.partial(relax_kernel, n_gz, n_gx),
        out_shape=(
            jax.ShapeDtypeStruct(rhs_field.shape, jnp.float32),
            jax.ShapeDtypeStruct((rows, chunks * width), jnp.float32),
        ),
        in_specs=[vmem, vmem, smem, smem, vmem],
        out_specs=(vmem, vmem),
        scratch_shapes=[slab] * 7
        + [
            planes(SOLVES, n_gz, 2),
            planes(n_gz, 4),
            planes(n_gz, 4),
            planes(n_gz + 1),
            planes(n_gz + 1),
            planes(4),
            planes(SOLVES),
            planes(SOLVES, 2),
            pltpu.VMEM((chunks * rows // 2, per_row * width), jnp.float32),
            pltpu.VMEM((rows, chunks, width), jnp.float32),
            pltpu.VMEM((rows, chunks, width), jnp.float32),
            pltpu.VMEM((rows, chunks, width), jnp.float32),
            sems(SOLVES, n_gz - 1),
            sems(SOLVES, n_gz - 1),
            sems(2, n_gz - 1),
            sems(2, n_gz - 1),
            sems(SOLVES, 2),
            sems(SOLVES, 2),
            sems(n_gx - 1),
            sems(n_gx - 1),
        ],
        compiler_params=pltpu.CompilerParams(
            collective_id=0, has_side_effects=True, vmem_limit_bytes=32 * 1024 * 1024
        ),
    )(rhs_field, heights.T, vert_coef, balance, pool)
    return pressure, coarse


def solution(mesh):
    placed = (P("gz", None, "gx"), P("gx", None), P(), P("gx", None))
    return jax.shard_map(
        functools.partial(on_device, mesh.shape["gz"], mesh.shape["gx"]),
        mesh=mesh,
        in_specs=placed,
        out_specs=(P("gz", None, "gx"), P("gx", "gz")),
        check_vma=False,
    )
```

```python
import functools

import jax
import jax.numpy as jnp
from jax import lax
from jax.experimental import pallas as pl
from jax.experimental.pallas import tpu as pltpu
from jax.sharding import PartitionSpec as P

SWEEPS = 2
SOLVES = 2 * SWEEPS
UNROLL = 8
MESH = pl.DeviceIdType.MESH


def relax_kernel(
    n_gz,
    n_gx,
    rhs_ref,
    heights_ref,
    coef_ref,
    balance_ref,
    pool_ref,
    p_ref,
    out_ref,
    side_inv,
    low_inv,
    upper,
    low_spike,
    up_spike,
    local,
    delta,
    ends,
    spikes,
    reduced,
    firsts,
    lasts,
    edge_spikes,
    halo_out,
    halo_in,
    pooled,
    bundles,
    outgoing,
    arrived,
    ends_send,
    ends_recv,
    spikes_send,
    spikes_recv,
    halo_send,
    halo_recv,
    tail_send,
    tail_recv,
):
    levels, rows, width = rhs_ref.shape
    total_z = coef_ref.shape[0]
    gz = lax.axis_index("gz")
    gx = lax.axis_index("gx")
    first_level = gz * levels

    barrier = pltpu.get_barrier_semaphore()
    for o in range(1, n_gz):
        pl.semaphore_signal(
            barrier, inc=1, device_id=(gx, lax.rem(gz + o, n_gz)), device_id_type=MESH
        )
    for o in range(1, n_gx):
        pl.semaphore_signal(
            barrier, inc=1, device_id=(lax.rem(gx + o, n_gx), gz), device_id_type=MESH
        )

    zero = jnp.zeros((rows, width), jnp.float32)
    one = jnp.ones((rows, width), jnp.float32)
    lane = lax.broadcasted_iota(jnp.int32, (rows, width), 1)
    row = lax.broadcasted_iota(jnp.int32, (rows, width), 0)
    parity = lax.rem(lane + row + gx * width, 2)
    at_left = lane == 0
    at_right = lane == width - 1
    at_top = row == 0
    at_bottom = row == rows - 1

    @pl.when(gx == 0)
    def _():
        for t in range(SOLVES):
            halo_in[t, 0] = zero

    @pl.when(gx == n_gx - 1)
    def _():
        for t in range(SOLVES):
            halo_in[t, 1] = zero

    def fluid_at(k):
        return (first_level + k >= heights_ref[...]).astype(jnp.float32)

    def factor(k, carry):
        up_before, d_before, spike_before = carry
        z = first_level + k
        below = coef_ref[z]
        above = jnp.where(z + 1 < total_z, coef_ref[jnp.minimum(z + 1, total_z - 1)], 0.0)
        fluid = fluid_at(k)
        low = -below * fluid
        centre = fluid * (4.0 + below + above) + (1.0 - fluid)
        inverse = 1.0 / (centre - low * up_before)
        up = -above * fluid * inverse
        low = low * inverse
        scale = fluid * inverse
        d = rhs_ref[k] * scale - low * d_before
        spike = -low * spike_before
        upper[k] = up
        low_inv[k] = low
        side_inv[k] = scale
        local[k] = d
        low_spike[k] = spike
        return up, d, spike

    def turned(cells, shift):
        shift = shift % width
        return cells if shift == 0 else pltpu.roll(cells, shift, 1)

    def around(cells, edge, edge_mask):
        left = jnp.where(at_left, 0.0, pltpu.roll(cells, 1, 1))
        right = jnp.where(at_right, 0.0, pltpu.roll(cells, width - 1, 1))
        up = jnp.where(at_top, 0.0, pltpu.roll(cells, 1, 0))
        down = jnp.where(at_bottom, 0.0, pltpu.roll(cells, rows - 1, 0))
        return (left + right) + (up + down) + jnp.where(edge_mask, edge, 0.0)

    def forward(edge_mask, step, carry):
        d, edges = carry
        for j in range(UNROLL):
            k = step * UNROLL + j
            side = rhs_ref[k] + around(p_ref[k], turned(edges, -j), edge_mask)
            d = side * side_inv[k] - low_inv[k] * d
            local[k] = d
        return d, turned(edges, -UNROLL)

    def with_edge(packed, cells, i, offset):
        return jnp.where(lane == i + offset, turned(cells, i + 1), packed)

    def factor_back(step, carry):
        g, low, high, g_edge, low_right, low_left, high_right, high_left = carry
        base = levels - UNROLL * (step + 1)
        g_edge, low_right, low_left, high_right, high_left = (
            turned(edge, UNROLL)
            for edge in (g_edge, low_right, low_left, high_right, high_left)
        )
        for i in reversed(range(UNROLL)):
            k = base + i
            up = upper[k]
            g = local[k] - up * g
            low = low_spike[k] - up * low
            high = -up * high
            local[k] = g
            low_spike[k] = low
            up_spike[k] = high
            g_edge = with_edge(g_edge, g, i, edge_lane(0))
            low_right = with_edge(low_right, low, i, 0)
            low_left = with_edge(low_left, low, i, 1)
            high_right = with_edge(high_right, high, i, 0)
            high_left = with_edge(high_left, high, i, 1)
        return g, low, high, g_edge, low_right, low_left, high_right, high_left

    def backward(offset, step, carry):
        g, g_edge = carry
        base = levels - UNROLL * (step + 1)
        g_edge = turned(g_edge, UNROLL)
        for i in reversed(range(UNROLL)):
            k = base + i
            g = local[k] - upper[k] * g
            local[k] = g
            g_edge = with_edge(g_edge, g, i, offset)
        return g, g_edge

    def from_left(colour):
        return lax.rem(row + gx * width, 2) == colour

    def edge_lane(colour):
        return jnp.where(from_left(colour), 1, 0)

    def halo_copies(t):
        to_right = pltpu.make_async_remote_copy(
            src_ref=halo_out.at[t],
            dst_ref=halo_in.at[t, 0],
            send_sem=halo_send.at[t, 0],
            recv_sem=halo_recv.at[t, 0],
            device_id=(lax.rem(gx + 1, n_gx), gz),
            device_id_type=MESH,
        )
        to_left = pltpu.make_async_remote_copy(
            src_ref=halo_out.at[t],
            dst_ref=halo_in.at[t, 1],
            send_sem=halo_send.at[t, 1],
            recv_sem=halo_recv.at[t, 1],
            device_id=(lax.rem(gx + n_gx - 1, n_gx), gz),
            device_id_type=MESH,
        )
        return to_right, to_left

    def start_halo(t):
        to_right, to_left = halo_copies(t)

        @pl.when(gx < n_gx - 1)
        def _():
            to_right.start()

        @pl.when(gx > 0)
        def _():
            to_left.start()

    def finish_halo(t, colour):
        to_right, to_left = halo_copies(t)

        @pl.when(gx > 0)
        def _():
            to_left.wait_send()
            to_right.wait_recv()

        @pl.when(gx < n_gx - 1)
        def _():
            to_right.wait_send()
            to_left.wait_recv()

        left_edge = halo_in[t, 0]
        right_edge = turned(halo_in[t, 1], -2)
        return jnp.where(from_left(colour), left_edge, right_edge)

    def column_copy(ref, send, recv, o):
        return pltpu.make_async_remote_copy(
            src_ref=ref,
            dst_ref=ref,
            send_sem=send.at[o - 1],
            recv_sem=recv.at[o - 1],
            device_id=(gx, lax.rem(gz + o, n_gz)),
            device_id_type=MESH,
        )

    for t in range(SOLVES):
        colour = t % 2
        if t == 0:
            lax.fori_loop(0, levels, factor, (zero, zero, one), unroll=UNROLL)
            d_last = local[levels - 1]
            spikes[gz, 0] = low_spike[levels - 1]
            spikes[gz, 1] = -upper[levels - 1]
            g, low, high, g_edge, *spike_edges = lax.fori_loop(
                0, levels // UNROLL, factor_back, (zero, zero, one) + (zero,) * 5
            )
            spikes[gz, 2] = low
            spikes[gz, 3] = high
            for e in range(4):
                edge_spikes[e] = spike_edges[e]
        else:
            edge_mask = (at_left | at_right) & (parity == colour)
            d_last, _ = lax.fori_loop(
                0,
                levels // UNROLL,
                functools.partial(forward, edge_mask),
                (zero, finish_halo(t - 1, colour)),
            )
            g, g_edge = lax.fori_loop(
                0,
                levels // UNROLL,
                functools.partial(backward, edge_lane(colour)),
                (zero, zero),
            )
        ends[t, gz] = jnp.where(parity == colour, g, turned(d_last, 1))
        copies = [
            column_copy(ends.at[t, gz], ends_send.at[t], ends_recv.at[t], o)
            for o in range(1, n_gz)
        ]
        if t == 0:
            copies += [
                column_copy(spikes.at[gz], spikes_send, spikes_recv, o) for o in range(1, n_gz)
            ]
            pl.semaphore_wait(barrier, n_gz + n_gx - 2)
        for copy in copies:
            copy.start()
        for copy in copies:
            copy.wait()

        if t == 0:
            beta = zero
            for s in range(n_gz):
                inverse = 1.0 / (1.0 - spikes[s, 2] * beta)
                reduced[s, 0] = beta
                reduced[s, 1] = inverse
                reduced[s, 2] = spikes[s, 3] * inverse
                beta = spikes[s, 1] + spikes[s, 0] * beta * reduced[s, 2]
                reduced[s, 3] = beta
        alpha = zero
        heads, tails = [], []
        for s in range(n_gz):
            both = ends[t, s]
            head = (both + spikes[s, 2] * alpha) * reduced[s, 1]
            alpha = turned(both, -1) + spikes[s, 0] * (alpha + reduced[s, 0] * head)
            heads.append(head)
            tails.append(alpha)
        after = zero
        firsts[n_gz] = zero
        lasts[0] = zero
        for s in reversed(range(n_gz)):
            lasts[s + 1] = tails[s] + reduced[s, 3] * after
            after = heads[s] + reduced[s, 2] * after
            firsts[s] = after
        below_value = lasts[gz]
        above_value = firsts[gz + 1]

        sent = from_left(colour)
        below_edge = jnp.where(sent, below_value[:, :1], below_value[:, width - 1 :])
        above_edge = jnp.where(sent, above_value[:, :1], above_value[:, width - 1 :])
        low_edge = jnp.where(sent, edge_spikes[1], edge_spikes[0])
        high_edge = jnp.where(sent, edge_spikes[3], edge_spikes[2])
        edge_cells = g_edge + low_edge * below_edge + high_edge * above_edge
        if t == SOLVES - 1:
            edge_cells = edge_cells - halo_out[t - 2]
        halo_out[t] = edge_cells
        start_halo(t)

        def correct(k, carry):
            value = local[k] + low_spike[k] * below_value + up_spike[k] * above_value
            before = zero if t == 0 else p_ref[k]
            cells = jnp.where(parity == colour, value, before)
            p_ref[k] = cells
            if t == SOLVES - 1:
                delta[k] = cells - before
            return carry

        lax.fori_loop(0, levels, correct, 0, unroll=UNROLL)

    edge_mask = (at_left | at_right) & (parity == 0)

    def coarsen(step, edges):
        for j in range(0, UNROLL, 2):
            k = step * UNROLL + j
            local[step * (UNROLL // 2) + j // 2] = fluid_at(k) * around(
                delta[k], turned(edges, -j), edge_mask
            ) + fluid_at(k + 1) * around(delta[k + 1], turned(edges, -j - 1), edge_mask)
        return turned(edges, -UNROLL)

    lax.fori_loop(0, levels // UNROLL, coarsen, finish_halo(SOLVES - 1, 0))

    half = rows // 2
    per_row = width // (width // 4)
    chunks = levels // 2 // per_row
    for i in range(levels // 2):
        c, part = i // per_row, i % per_row
        pooled[c * half : (c + 1) * half, part * width : (part + 1) * width] = (
            local[i, pl.ds(0, half, 2), :] + local[i, pl.ds(1, half, 2), :]
        )
    packed = jnp.dot(
        pooled[...],
        pool_ref[...],
        preferred_element_type=jnp.float32,
        precision=lax.Precision.HIGHEST,
    )
    for c in range(chunks):
        for h in range(2):
            bundles[h * half : (h + 1) * half, c, :] = packed[
                c * half : (c + 1) * half, h * width : (h + 1) * width
            ]
    share = rows // n_gx
    for j in range(rows):
        b = balance_ref[0, j]
        outgoing[j] = bundles[(b & 1) * half + (b >> 1)]
    copies = []
    for o in range(1, n_gx):
        owner = lax.rem(gx + o, n_gx)
        copies.append(
            pltpu.make_async_remote_copy(
                src_ref=outgoing.at[pl.ds(owner * share, share)],
                dst_ref=arrived.at[pl.ds(gx * share, share)],
                send_sem=tail_send.at[o - 1],
                recv_sem=tail_recv.at[o - 1],
                device_id=(owner, gz),
                device_id_type=MESH,
            )
        )
    for copy in copies:
        copy.start()
    arrived[pl.ds(gx * share, share)] = outgoing[pl.ds(gx * share, share)]
    for copy in copies:
        copy.wait()
    for c in range(chunks):
        out_ref[:, c * width : (c + 1) * width] = arrived[:, c, :]


def on_device(n_gz, n_gx, rhs_field, heights, vert_coef, balance):
    levels, rows, width = rhs_field.shape
    per_row = 4
    chunks = levels // 2 // per_row
    spot = jnp.arange(per_row * width, dtype=jnp.int32)[:, None]
    target = jnp.arange(2 * width, dtype=jnp.int32)[None, :]
    quarter = width // 4
    coarse_x = (spot % width) // 2
    pool = jnp.where(
        (target // width == coarse_x // quarter)
        & (target % width == (spot // width) * quarter + coarse_x % quarter),
        0.125,
        0.0,
    ).astype(jnp.float32)
    vmem = pl.BlockSpec(memory_space=pltpu.VMEM)
    smem = pl.BlockSpec(memory_space=pltpu.SMEM)
    slab = pltpu.VMEM((levels, rows, width), jnp.float32)
    plane = (rows, width)

    def planes(*lead):
        return pltpu.VMEM(lead + plane, jnp.float32)

    def sems(*lead):
        return pltpu.SemaphoreType.DMA(lead)

    pressure, coarse = pl.pallas_call(
        functools.partial(relax_kernel, n_gz, n_gx),
        out_shape=(
            jax.ShapeDtypeStruct(rhs_field.shape, jnp.float32),
            jax.ShapeDtypeStruct((rows, chunks * width), jnp.float32),
        ),
        in_specs=[vmem, vmem, smem, smem, vmem],
        out_specs=(vmem, vmem),
        scratch_shapes=[slab] * 7
        + [
            planes(SOLVES, n_gz),
            planes(n_gz, 4),
            planes(n_gz, 4),
            planes(n_gz + 1),
            planes(n_gz + 1),
            planes(4),
            planes(SOLVES),
            planes(SOLVES, 2),
            pltpu.VMEM((chunks * rows // 2, per_row * width), jnp.float32),
            pltpu.VMEM((rows, chunks, width), jnp.float32),
            pltpu.VMEM((rows, chunks, width), jnp.float32),
            pltpu.VMEM((rows, chunks, width), jnp.float32),
            sems(SOLVES, n_gz - 1),
            sems(SOLVES, n_gz - 1),
            sems(n_gz - 1),
            sems(n_gz - 1),
            sems(SOLVES, 2),
            sems(SOLVES, 2),
            sems(n_gx - 1),
            sems(n_gx - 1),
        ],
        compiler_params=pltpu.CompilerParams(
            collective_id=0, has_side_effects=True, vmem_limit_bytes=32 * 1024 * 1024
        ),
    )(rhs_field, heights.T, vert_coef, balance, pool)
    return pressure, coarse


def solution(mesh):
    placed = (P("gz", None, "gx"), P("gx", None), P(), P("gx", None))
    return jax.shard_map(
        functools.partial(on_device, mesh.shape["gz"], mesh.shape["gx"]),
        mesh=mesh,
        in_specs=placed,
        out_specs=(P("gz", None, "gx"), P("gx", "gz")),
        check_vma=False,
    )
```

```python
import functools

import jax
import jax.numpy as jnp
from jax import lax
from jax.experimental import pallas as pl
from jax.experimental.pallas import tpu as pltpu
from jax.sharding import PartitionSpec as P

SWEEPS = 2
SOLVES = 2 * SWEEPS
UNROLL = 8
MESH = pl.DeviceIdType.MESH


def relax_kernel(
    n_gz,
    n_gx,
    rhs_ref,
    heights_ref,
    coef_ref,
    balance_ref,
    pool_ref,
    p_ref,
    out_ref,
    side_inv,
    low_inv,
    upper,
    low_spike,
    up_spike,
    local,
    delta,
    ends,
    spikes,
    reduced,
    firsts,
    lasts,
    edge_spikes,
    halo_out,
    halo_in,
    pooled,
    bundles,
    outgoing,
    arrived,
    ends_send,
    ends_recv,
    spikes_send,
    spikes_recv,
    halo_send,
    halo_recv,
    tail_send,
    tail_recv,
):
    levels, rows, width = rhs_ref.shape
    total_z = coef_ref.shape[0]
    gz = lax.axis_index("gz")
    gx = lax.axis_index("gx")
    first_level = gz * levels

    barrier = pltpu.get_barrier_semaphore()
    for o in range(1, n_gz):
        pl.semaphore_signal(
            barrier, inc=1, device_id=(gx, lax.rem(gz + o, n_gz)), device_id_type=MESH
        )
    for o in range(1, n_gx):
        pl.semaphore_signal(
            barrier, inc=1, device_id=(lax.rem(gx + o, n_gx), gz), device_id_type=MESH
        )

    zero = jnp.zeros((rows, width), jnp.float32)
    one = jnp.ones((rows, width), jnp.float32)
    lane = lax.broadcasted_iota(jnp.int32, (rows, width), 1)
    row = lax.broadcasted_iota(jnp.int32, (rows, width), 0)
    parity = lax.rem(lane + row + gx * width, 2)
    at_left = lane == 0
    at_right = lane == width - 1
    at_top = row == 0
    at_bottom = row == rows - 1

    @pl.when(gx == 0)
    def _():
        for t in range(SOLVES):
            halo_in[t, 0] = zero

    @pl.when(gx == n_gx - 1)
    def _():
        for t in range(SOLVES):
            halo_in[t, 1] = zero

    def fluid_at(k):
        return (first_level + k >= heights_ref[...]).astype(jnp.float32)

    def factor(k, carry):
        up_before, d_before, spike_before = carry
        z = first_level + k
        below = coef_ref[z]
        above = jnp.where(z + 1 < total_z, coef_ref[jnp.minimum(z + 1, total_z - 1)], 0.0)
        fluid = fluid_at(k)
        low = -below * fluid
        centre = fluid * (4.0 + below + above) + (1.0 - fluid)
        inverse = 1.0 / (centre - low * up_before)
        up = -above * fluid * inverse
        low = low * inverse
        scale = fluid * inverse
        d = rhs_ref[k] * scale - low * d_before
        spike = -low * spike_before
        upper[k] = up
        low_inv[k] = low
        side_inv[k] = scale
        local[k] = d
        low_spike[k] = spike
        return up, d, spike

    def turned(cells, shift):
        shift = shift % width
        return cells if shift == 0 else pltpu.roll(cells, shift, 1)

    def around(cells, edge, edge_mask):
        left = jnp.where(at_left, 0.0, pltpu.roll(cells, 1, 1))
        right = jnp.where(at_right, 0.0, pltpu.roll(cells, width - 1, 1))
        up = jnp.where(at_top, 0.0, pltpu.roll(cells, 1, 0))
        down = jnp.where(at_bottom, 0.0, pltpu.roll(cells, rows - 1, 0))
        return (left + right) + (up + down) + jnp.where(edge_mask, edge, 0.0)

    def forward(edge_mask, step, carry):
        d, edges = carry
        for j in range(UNROLL):
            k = step * UNROLL + j
            side = rhs_ref[k] + around(p_ref[k], turned(edges, -j), edge_mask)
            d = side * side_inv[k] - low_inv[k] * d
            local[k] = d
        return d, turned(edges, -UNROLL)

    def with_edge(packed, cells, i, offset):
        return jnp.where(lane == i + offset, turned(cells, i + 1), packed)

    def factor_back(step, carry):
        g, low, high, g_edge, low_right, low_left, high_right, high_left = carry
        base = levels - UNROLL * (step + 1)
        g_edge, low_right, low_left, high_right, high_left = (
            turned(edge, UNROLL)
            for edge in (g_edge, low_right, low_left, high_right, high_left)
        )
        for i in reversed(range(UNROLL)):
            k = base + i
            up = upper[k]
            g = local[k] - up * g
            low = low_spike[k] - up * low
            high = -up * high
            local[k] = g
            low_spike[k] = low
            up_spike[k] = high
            g_edge = with_edge(g_edge, g, i, edge_lane(0))
            low_right = with_edge(low_right, low, i, 0)
            low_left = with_edge(low_left, low, i, 1)
            high_right = with_edge(high_right, high, i, 0)
            high_left = with_edge(high_left, high, i, 1)
        return g, low, high, g_edge, low_right, low_left, high_right, high_left

    def backward(offset, step, carry):
        g, g_edge = carry
        base = levels - UNROLL * (step + 1)
        g_edge = turned(g_edge, UNROLL)
        for i in reversed(range(UNROLL)):
            k = base + i
            g = local[k] - upper[k] * g
            local[k] = g
            g_edge = with_edge(g_edge, g, i, offset)
        return g, g_edge

    def from_left(colour):
        return lax.rem(row + gx * width, 2) == colour

    def edge_lane(colour):
        return jnp.where(from_left(colour), 1, 0)

    def halo_copies(t):
        to_right = pltpu.make_async_remote_copy(
            src_ref=halo_out.at[t],
            dst_ref=halo_in.at[t, 0],
            send_sem=halo_send.at[t, 0],
            recv_sem=halo_recv.at[t, 0],
            device_id=(lax.rem(gx + 1, n_gx), gz),
            device_id_type=MESH,
        )
        to_left = pltpu.make_async_remote_copy(
            src_ref=halo_out.at[t],
            dst_ref=halo_in.at[t, 1],
            send_sem=halo_send.at[t, 1],
            recv_sem=halo_recv.at[t, 1],
            device_id=(lax.rem(gx + n_gx - 1, n_gx), gz),
            device_id_type=MESH,
        )
        return to_right, to_left

    def start_halo(t):
        to_right, to_left = halo_copies(t)

        @pl.when(gx < n_gx - 1)
        def _():
            to_right.start()

        @pl.when(gx > 0)
        def _():
            to_left.start()

    def finish_halo(t, colour):
        to_right, to_left = halo_copies(t)

        @pl.when(gx > 0)
        def _():
            to_left.wait_send()
            to_right.wait_recv()

        @pl.when(gx < n_gx - 1)
        def _():
            to_right.wait_send()
            to_left.wait_recv()

        left_edge = halo_in[t, 0]
        right_edge = turned(halo_in[t, 1], -2)
        return jnp.where(from_left(colour), left_edge, right_edge)

    def column_copy(ref, send, recv, o):
        return pltpu.make_async_remote_copy(
            src_ref=ref,
            dst_ref=ref,
            send_sem=send.at[o - 1],
            recv_sem=recv.at[o - 1],
            device_id=(gx, lax.rem(gz + o, n_gz)),
            device_id_type=MESH,
        )

    for t in range(SOLVES):
        colour = t % 2
        if t == 0:
            lax.fori_loop(0, levels, factor, (zero, zero, one), unroll=UNROLL)
            d_last = local[levels - 1]
            spikes[gz, 0] = low_spike[levels - 1]
            spikes[gz, 1] = -upper[levels - 1]
            pl.semaphore_wait(barrier, n_gz + n_gx - 2)
            early = [
                column_copy(
                    spikes.at[gz, pl.ds(0, 2)], spikes_send.at[0], spikes_recv.at[0], o
                )
                for o in range(1, n_gz)
            ]
            for copy in early:
                copy.start()
            g, low, high, g_edge, *spike_edges = lax.fori_loop(
                0, levels // UNROLL, factor_back, (zero, zero, one) + (zero,) * 5
            )
            spikes[gz, 2] = low
            spikes[gz, 3] = high
            for e in range(4):
                edge_spikes[e] = spike_edges[e]
        else:
            edge_mask = (at_left | at_right) & (parity == colour)
            d_last, _ = lax.fori_loop(
                0,
                levels // UNROLL,
                functools.partial(forward, edge_mask),
                (zero, finish_halo(t - 1, colour)),
            )
            g, g_edge = lax.fori_loop(
                0,
                levels // UNROLL,
                functools.partial(backward, edge_lane(colour)),
                (zero, zero),
            )
        ends[t, gz] = jnp.where(parity == colour, g, turned(d_last, 1))
        copies = [
            column_copy(ends.at[t, gz], ends_send.at[t], ends_recv.at[t], o)
            for o in range(1, n_gz)
        ]
        if t == 0:
            copies += [
                column_copy(
                    spikes.at[gz, pl.ds(2, 2)], spikes_send.at[1], spikes_recv.at[1], o
                )
                for o in range(1, n_gz)
            ]
        for copy in copies:
            copy.start()
        if t == 0:
            copies += early
        for copy in copies:
            copy.wait()

        if t == 0:
            beta = zero
            for s in range(n_gz):
                inverse = 1.0 / (1.0 - spikes[s, 2] * beta)
                reduced[s, 0] = beta
                reduced[s, 1] = inverse
                reduced[s, 2] = spikes[s, 3] * inverse
                beta = spikes[s, 1] + spikes[s, 0] * beta * reduced[s, 2]
                reduced[s, 3] = beta
        alpha = zero
        heads, tails = [], []
        for s in range(n_gz):
            both = ends[t, s]
            head = (both + spikes[s, 2] * alpha) * reduced[s, 1]
            alpha = turned(both, -1) + spikes[s, 0] * (alpha + reduced[s, 0] * head)
            heads.append(head)
            tails.append(alpha)
        after = zero
        firsts[n_gz] = zero
        lasts[0] = zero
        for s in reversed(range(n_gz)):
            lasts[s + 1] = tails[s] + reduced[s, 3] * after
            after = heads[s] + reduced[s, 2] * after
            firsts[s] = after
        below_value = lasts[gz]
        above_value = firsts[gz + 1]

        sent = from_left(colour)
        below_edge = jnp.where(sent, below_value[:, :1], below_value[:, width - 1 :])
        above_edge = jnp.where(sent, above_value[:, :1], above_value[:, width - 1 :])
        low_edge = jnp.where(sent, edge_spikes[1], edge_spikes[0])
        high_edge = jnp.where(sent, edge_spikes[3], edge_spikes[2])
        edge_cells = g_edge + low_edge * below_edge + high_edge * above_edge
        if t == SOLVES - 1:
            edge_cells = edge_cells - halo_out[t - 2]
        halo_out[t] = edge_cells
        start_halo(t)

        def correct(k, carry):
            value = local[k] + low_spike[k] * below_value + up_spike[k] * above_value
            before = zero if t == 0 else p_ref[k]
            cells = jnp.where(parity == colour, value, before)
            p_ref[k] = cells
            if t == SOLVES - 1:
                delta[k] = cells - before
            return carry

        lax.fori_loop(0, levels, correct, 0, unroll=UNROLL)

    edge_mask = (at_left | at_right) & (parity == 0)

    def coarsen(step, edges):
        for j in range(0, UNROLL, 2):
            k = step * UNROLL + j
            local[step * (UNROLL // 2) + j // 2] = fluid_at(k) * around(
                delta[k], turned(edges, -j), edge_mask
            ) + fluid_at(k + 1) * around(delta[k + 1], turned(edges, -j - 1), edge_mask)
        return turned(edges, -UNROLL)

    lax.fori_loop(0, levels // UNROLL, coarsen, finish_halo(SOLVES - 1, 0))

    half = rows // 2
    per_row = width // (width // 4)
    chunks = levels // 2 // per_row
    for i in range(levels // 2):
        c, part = i // per_row, i % per_row
        pooled[c * half : (c + 1) * half, part * width : (part + 1) * width] = (
            local[i, pl.ds(0, half, 2), :] + local[i, pl.ds(1, half, 2), :]
        )
    packed = jnp.dot(
        pooled[...],
        pool_ref[...],
        preferred_element_type=jnp.float32,
        precision=lax.Precision.HIGHEST,
    )
    for c in range(chunks):
        for h in range(2):
            bundles[h * half : (h + 1) * half, c, :] = packed[
                c * half : (c + 1) * half, h * width : (h + 1) * width
            ]
    share = rows // n_gx
    for j in range(rows):
        b = balance_ref[0, j]
        outgoing[j] = bundles[(b & 1) * half + (b >> 1)]
    copies = []
    for o in range(1, n_gx):
        owner = lax.rem(gx + o, n_gx)
        copies.append(
            pltpu.make_async_remote_copy(
                src_ref=outgoing.at[pl.ds(owner * share, share)],
                dst_ref=arrived.at[pl.ds(gx * share, share)],
                send_sem=tail_send.at[o - 1],
                recv_sem=tail_recv.at[o - 1],
                device_id=(owner, gz),
                device_id_type=MESH,
            )
        )
    for copy in copies:
        copy.start()
    arrived[pl.ds(gx * share, share)] = outgoing[pl.ds(gx * share, share)]
    for copy in copies:
        copy.wait()
    for c in range(chunks):
        out_ref[:, c * width : (c + 1) * width] = arrived[:, c, :]


def on_device(n_gz, n_gx, rhs_field, heights, vert_coef, balance):
    levels, rows, width = rhs_field.shape
    per_row = 4
    chunks = levels // 2 // per_row
    spot = jnp.arange(per_row * width, dtype=jnp.int32)[:, None]
    target = jnp.arange(2 * width, dtype=jnp.int32)[None, :]
    quarter = width // 4
    coarse_x = (spot % width) // 2
    pool = jnp.where(
        (target // width == coarse_x // quarter)
        & (target % width == (spot // width) * quarter + coarse_x % quarter),
        0.125,
        0.0,
    ).astype(jnp.float32)
    vmem = pl.BlockSpec(memory_space=pltpu.VMEM)
    smem = pl.BlockSpec(memory_space=pltpu.SMEM)
    slab = pltpu.VMEM((levels, rows, width), jnp.float32)
    plane = (rows, width)

    def planes(*lead):
        return pltpu.VMEM(lead + plane, jnp.float32)

    def sems(*lead):
        return pltpu.SemaphoreType.DMA(lead)

    pressure, coarse = pl.pallas_call(
        functools.partial(relax_kernel, n_gz, n_gx),
        out_shape=(
            jax.ShapeDtypeStruct(rhs_field.shape, jnp.float32),
            jax.ShapeDtypeStruct((rows, chunks * width), jnp.float32),
        ),
        in_specs=[vmem, vmem, smem, smem, vmem],
        out_specs=(vmem, vmem),
        scratch_shapes=[slab] * 7
        + [
            planes(SOLVES, n_gz),
            planes(n_gz, 4),
            planes(n_gz, 4),
            planes(n_gz + 1),
            planes(n_gz + 1),
            planes(4),
            planes(SOLVES),
            planes(SOLVES, 2),
            pltpu.VMEM((chunks * rows // 2, per_row * width), jnp.float32),
            pltpu.VMEM((rows, chunks, width), jnp.float32),
            pltpu.VMEM((rows, chunks, width), jnp.float32),
            pltpu.VMEM((rows, chunks, width), jnp.float32),
            sems(SOLVES, n_gz - 1),
            sems(SOLVES, n_gz - 1),
            sems(2, n_gz - 1),
            sems(2, n_gz - 1),
            sems(SOLVES, 2),
            sems(SOLVES, 2),
            sems(n_gx - 1),
            sems(n_gx - 1),
        ],
        compiler_params=pltpu.CompilerParams(
            collective_id=0, has_side_effects=True, vmem_limit_bytes=32 * 1024 * 1024
        ),
    )(rhs_field, heights.T, vert_coef, balance, pool)
    return pressure, coarse


def solution(mesh):
    placed = (P("gz", None, "gx"), P("gx", None), P(), P("gx", None))
    return jax.shard_map(
        functools.partial(on_device, mesh.shape["gz"], mesh.shape["gx"]),
        mesh=mesh,
        in_specs=placed,
        out_specs=(P("gz", None, "gx"), P("gx", "gz")),
        check_vma=False,
    )
```

```python
import functools

import jax
import jax.numpy as jnp
from jax import lax
from jax.experimental import pallas as pl
from jax.experimental.pallas import tpu as pltpu
from jax.sharding import PartitionSpec as P

SWEEPS = 2
SOLVES = 2 * SWEEPS
UNROLL = 8
MESH = pl.DeviceIdType.MESH


def relax_kernel(
    n_gz,
    n_gx,
    rhs_ref,
    heights_ref,
    coef_ref,
    balance_ref,
    pool_ref,
    p_ref,
    out_ref,
    side_inv,
    low_inv,
    upper,
    low_spike,
    up_spike,
    local,
    delta,
    ends,
    spikes,
    reduced,
    firsts,
    lasts,
    edge_spikes,
    halo_out,
    halo_in,
    pooled,
    bundles,
    outgoing,
    arrived,
    ends_send,
    ends_recv,
    spikes_send,
    spikes_recv,
    halo_send,
    halo_recv,
    tail_send,
    tail_recv,
):
    levels, rows, width = rhs_ref.shape
    total_z = coef_ref.shape[0]
    gz = lax.axis_index("gz")
    gx = lax.axis_index("gx")
    first_level = gz * levels

    barrier = pltpu.get_barrier_semaphore()
    for o in range(1, n_gz):
        pl.semaphore_signal(
            barrier, inc=1, device_id=(gx, lax.rem(gz + o, n_gz)), device_id_type=MESH
        )
    for o in range(1, n_gx):
        pl.semaphore_signal(
            barrier, inc=1, device_id=(lax.rem(gx + o, n_gx), gz), device_id_type=MESH
        )

    zero = jnp.zeros((rows, width), jnp.float32)
    one = jnp.ones((rows, width), jnp.float32)
    lane = lax.broadcasted_iota(jnp.int32, (rows, width), 1)
    row = lax.broadcasted_iota(jnp.int32, (rows, width), 0)
    parity = lax.rem(lane + row + gx * width, 2)
    at_left = lane == 0
    at_right = lane == width - 1
    at_top = row == 0
    at_bottom = row == rows - 1

    @pl.when(gx == 0)
    def _():
        for t in range(SOLVES):
            halo_in[t, 0] = zero

    @pl.when(gx == n_gx - 1)
    def _():
        for t in range(SOLVES):
            halo_in[t, 1] = zero

    def fluid_at(k):
        return (first_level + k >= heights_ref[...]).astype(jnp.float32)

    def factor(k, carry):
        up_before, d_before, spike_before = carry
        z = first_level + k
        below = coef_ref[z]
        above = jnp.where(z + 1 < total_z, coef_ref[jnp.minimum(z + 1, total_z - 1)], 0.0)
        fluid = fluid_at(k)
        low = -below * fluid
        centre = fluid * (4.0 + below + above) + (1.0 - fluid)
        inverse = 1.0 / (centre - low * up_before)
        up = -above * fluid * inverse
        low = low * inverse
        scale = fluid * inverse
        d = rhs_ref[k] * scale - low * d_before
        spike = -low * spike_before
        upper[k] = up
        low_inv[k] = low
        side_inv[k] = scale
        local[k] = d
        low_spike[k] = spike
        return up, d, spike

    def turned(cells, shift):
        shift = shift % width
        return cells if shift == 0 else pltpu.roll(cells, shift, 1)

    def around(cells, edge, edge_mask):
        left = jnp.where(at_left, 0.0, pltpu.roll(cells, 1, 1))
        right = jnp.where(at_right, 0.0, pltpu.roll(cells, width - 1, 1))
        up = jnp.where(at_top, 0.0, pltpu.roll(cells, 1, 0))
        down = jnp.where(at_bottom, 0.0, pltpu.roll(cells, rows - 1, 0))
        return (left + right) + (up + down) + jnp.where(edge_mask, edge, 0.0)

    def forward(edge_mask, step, carry):
        d, edges = carry
        for j in range(UNROLL):
            k = step * UNROLL + j
            side = rhs_ref[k] + around(p_ref[k], turned(edges, -j), edge_mask)
            d = side * side_inv[k] - low_inv[k] * d
            local[k] = d
        return d, turned(edges, -UNROLL)

    def with_edge(packed, cells, i, offset):
        return jnp.where(lane == i + offset, turned(cells, i + 1), packed)

    def factor_back(step, carry):
        g, low, high, g_edge, low_right, low_left, high_right, high_left = carry
        base = levels - UNROLL * (step + 1)
        g_edge, low_right, low_left, high_right, high_left = (
            turned(edge, UNROLL)
            for edge in (g_edge, low_right, low_left, high_right, high_left)
        )
        for i in reversed(range(UNROLL)):
            k = base + i
            up = upper[k]
            g = local[k] - up * g
            low = low_spike[k] - up * low
            high = -up * high
            local[k] = g
            low_spike[k] = low
            up_spike[k] = high
            g_edge = with_edge(g_edge, g, i, edge_lane(0))
            low_right = with_edge(low_right, low, i, 0)
            low_left = with_edge(low_left, low, i, 1)
            high_right = with_edge(high_right, high, i, 0)
            high_left = with_edge(high_left, high, i, 1)
        return g, low, high, g_edge, low_right, low_left, high_right, high_left

    def backward(offset, step, carry):
        g, g_edge = carry
        base = levels - UNROLL * (step + 1)
        g_edge = turned(g_edge, UNROLL)
        for i in reversed(range(UNROLL)):
            k = base + i
            g = local[k] - upper[k] * g
            local[k] = g
            g_edge = with_edge(g_edge, g, i, offset)
        return g, g_edge

    def from_left(colour):
        return lax.rem(row + gx * width, 2) == colour

    def edge_lane(colour):
        return jnp.where(from_left(colour), 1, 0)

    def halo_copies(t):
        to_right = pltpu.make_async_remote_copy(
            src_ref=halo_out.at[t],
            dst_ref=halo_in.at[t, 0],
            send_sem=halo_send.at[t, 0],
            recv_sem=halo_recv.at[t, 0],
            device_id=(lax.rem(gx + 1, n_gx), gz),
            device_id_type=MESH,
        )
        to_left = pltpu.make_async_remote_copy(
            src_ref=halo_out.at[t],
            dst_ref=halo_in.at[t, 1],
            send_sem=halo_send.at[t, 1],
            recv_sem=halo_recv.at[t, 1],
            device_id=(lax.rem(gx + n_gx - 1, n_gx), gz),
            device_id_type=MESH,
        )
        return to_right, to_left

    def start_halo(t):
        to_right, to_left = halo_copies(t)

        @pl.when(gx < n_gx - 1)
        def _():
            to_right.start()

        @pl.when(gx > 0)
        def _():
            to_left.start()

    def finish_halo(t, colour):
        to_right, to_left = halo_copies(t)

        @pl.when(gx > 0)
        def _():
            to_left.wait_send()
            to_right.wait_recv()

        @pl.when(gx < n_gx - 1)
        def _():
            to_right.wait_send()
            to_left.wait_recv()

        left_edge = halo_in[t, 0]
        right_edge = turned(halo_in[t, 1], -2)
        return jnp.where(from_left(colour), left_edge, right_edge)

    def column_copy(ref, send, recv, o):
        return pltpu.make_async_remote_copy(
            src_ref=ref,
            dst_ref=ref,
            send_sem=send.at[o - 1],
            recv_sem=recv.at[o - 1],
            device_id=(gx, lax.rem(gz + o, n_gz)),
            device_id_type=MESH,
        )

    for t in range(SOLVES):
        colour = t % 2
        if t == 0:
            lax.fori_loop(0, levels, factor, (zero, zero, one), unroll=UNROLL)
            d_last = local[levels - 1]
            spikes[gz, 0] = low_spike[levels - 1]
            spikes[gz, 1] = -upper[levels - 1]
            pl.semaphore_wait(barrier, n_gz + n_gx - 2)
            early = [
                column_copy(
                    spikes.at[gz, pl.ds(0, 2)], spikes_send.at[0], spikes_recv.at[0], o
                )
                for o in range(1, n_gz)
            ]
            for copy in early:
                copy.start()
            g, low, high, g_edge, *spike_edges = lax.fori_loop(
                0, levels // UNROLL, factor_back, (zero, zero, one) + (zero,) * 5
            )
            spikes[gz, 2] = low
            spikes[gz, 3] = high
            for e in range(4):
                edge_spikes[e] = spike_edges[e]
        else:
            edge_mask = (at_left | at_right) & (parity == colour)
            d_last, _ = lax.fori_loop(
                0,
                levels // UNROLL,
                functools.partial(forward, edge_mask),
                (zero, finish_halo(t - 1, colour)),
            )
            g, g_edge = lax.fori_loop(
                0,
                levels // UNROLL,
                functools.partial(backward, edge_lane(colour)),
                (zero, zero),
            )
        ends[t, gz] = jnp.where(parity == colour, g, turned(d_last, 1))
        copies = [
            column_copy(ends.at[t, gz], ends_send.at[t], ends_recv.at[t], o)
            for o in range(1, n_gz)
        ]
        if t == 0:
            copies += [
                column_copy(
                    spikes.at[gz, pl.ds(2, 2)], spikes_send.at[1], spikes_recv.at[1], o
                )
                for o in range(1, n_gz)
            ]
        for copy in copies:
            copy.start()
        if t == 0:
            copies += early
        for copy in copies:
            copy.wait_recv()

        if t == 0:
            beta = zero
            for s in range(n_gz):
                inverse = 1.0 / (1.0 - spikes[s, 2] * beta)
                reduced[s, 0] = beta
                reduced[s, 1] = inverse
                reduced[s, 2] = spikes[s, 3] * inverse
                beta = spikes[s, 1] + spikes[s, 0] * beta * reduced[s, 2]
                reduced[s, 3] = beta
        alpha = zero
        heads, tails = [], []
        for s in range(n_gz):
            both = ends[t, s]
            head = (both + spikes[s, 2] * alpha) * reduced[s, 1]
            alpha = turned(both, -1) + spikes[s, 0] * (alpha + reduced[s, 0] * head)
            heads.append(head)
            tails.append(alpha)
        after = zero
        firsts[n_gz] = zero
        lasts[0] = zero
        for s in reversed(range(n_gz)):
            lasts[s + 1] = tails[s] + reduced[s, 3] * after
            after = heads[s] + reduced[s, 2] * after
            firsts[s] = after
        below_value = lasts[gz]
        above_value = firsts[gz + 1]

        sent = from_left(colour)
        below_edge = jnp.where(sent, below_value[:, :1], below_value[:, width - 1 :])
        above_edge = jnp.where(sent, above_value[:, :1], above_value[:, width - 1 :])
        low_edge = jnp.where(sent, edge_spikes[1], edge_spikes[0])
        high_edge = jnp.where(sent, edge_spikes[3], edge_spikes[2])
        edge_cells = g_edge + low_edge * below_edge + high_edge * above_edge
        if t == SOLVES - 1:
            edge_cells = edge_cells - halo_out[t - 2]
        halo_out[t] = edge_cells
        start_halo(t)

        def correct(k, carry):
            value = local[k] + low_spike[k] * below_value + up_spike[k] * above_value
            before = zero if t == 0 else p_ref[k]
            cells = jnp.where(parity == colour, value, before)
            p_ref[k] = cells
            if t == SOLVES - 1:
                delta[k] = cells - before
            return carry

        lax.fori_loop(0, levels, correct, 0, unroll=UNROLL)
        for copy in copies:
            copy.wait_send()

    edge_mask = (at_left | at_right) & (parity == 0)

    def coarsen(step, edges):
        for j in range(0, UNROLL, 2):
            k = step * UNROLL + j
            local[step * (UNROLL // 2) + j // 2] = fluid_at(k) * around(
                delta[k], turned(edges, -j), edge_mask
            ) + fluid_at(k + 1) * around(delta[k + 1], turned(edges, -j - 1), edge_mask)
        return turned(edges, -UNROLL)

    lax.fori_loop(0, levels // UNROLL, coarsen, finish_halo(SOLVES - 1, 0))

    half = rows // 2
    per_row = width // (width // 4)
    chunks = levels // 2 // per_row
    for i in range(levels // 2):
        c, part = i // per_row, i % per_row
        pooled[c * half : (c + 1) * half, part * width : (part + 1) * width] = (
            local[i, pl.ds(0, half, 2), :] + local[i, pl.ds(1, half, 2), :]
        )
    packed = jnp.dot(
        pooled[...],
        pool_ref[...],
        preferred_element_type=jnp.float32,
        precision=lax.Precision.HIGHEST,
    )
    for c in range(chunks):
        for h in range(2):
            bundles[h * half : (h + 1) * half, c, :] = packed[
                c * half : (c + 1) * half, h * width : (h + 1) * width
            ]
    share = rows // n_gx
    for j in range(rows):
        b = balance_ref[0, j]
        outgoing[j] = bundles[(b & 1) * half + (b >> 1)]
    copies = []
    for o in range(1, n_gx):
        owner = lax.rem(gx + o, n_gx)
        copies.append(
            pltpu.make_async_remote_copy(
                src_ref=outgoing.at[pl.ds(owner * share, share)],
                dst_ref=arrived.at[pl.ds(gx * share, share)],
                send_sem=tail_send.at[o - 1],
                recv_sem=tail_recv.at[o - 1],
                device_id=(owner, gz),
                device_id_type=MESH,
            )
        )
    for copy in copies:
        copy.start()
    arrived[pl.ds(gx * share, share)] = outgoing[pl.ds(gx * share, share)]
    for copy in copies:
        copy.wait()
    for c in range(chunks):
        out_ref[:, c * width : (c + 1) * width] = arrived[:, c, :]


def on_device(n_gz, n_gx, rhs_field, heights, vert_coef, balance):
    levels, rows, width = rhs_field.shape
    per_row = 4
    chunks = levels // 2 // per_row
    spot = jnp.arange(per_row * width, dtype=jnp.int32)[:, None]
    target = jnp.arange(2 * width, dtype=jnp.int32)[None, :]
    quarter = width // 4
    coarse_x = (spot % width) // 2
    pool = jnp.where(
        (target // width == coarse_x // quarter)
        & (target % width == (spot // width) * quarter + coarse_x % quarter),
        0.125,
        0.0,
    ).astype(jnp.float32)
    vmem = pl.BlockSpec(memory_space=pltpu.VMEM)
    smem = pl.BlockSpec(memory_space=pltpu.SMEM)
    slab = pltpu.VMEM((levels, rows, width), jnp.float32)
    plane = (rows, width)

    def planes(*lead):
        return pltpu.VMEM(lead + plane, jnp.float32)

    def sems(*lead):
        return pltpu.SemaphoreType.DMA(lead)

    pressure, coarse = pl.pallas_call(
        functools.partial(relax_kernel, n_gz, n_gx),
        out_shape=(
            jax.ShapeDtypeStruct(rhs_field.shape, jnp.float32),
            jax.ShapeDtypeStruct((rows, chunks * width), jnp.float32),
        ),
        in_specs=[vmem, vmem, smem, smem, vmem],
        out_specs=(vmem, vmem),
        scratch_shapes=[slab] * 7
        + [
            planes(SOLVES, n_gz),
            planes(n_gz, 4),
            planes(n_gz, 4),
            planes(n_gz + 1),
            planes(n_gz + 1),
            planes(4),
            planes(SOLVES),
            planes(SOLVES, 2),
            pltpu.VMEM((chunks * rows // 2, per_row * width), jnp.float32),
            pltpu.VMEM((rows, chunks, width), jnp.float32),
            pltpu.VMEM((rows, chunks, width), jnp.float32),
            pltpu.VMEM((rows, chunks, width), jnp.float32),
            sems(SOLVES, n_gz - 1),
            sems(SOLVES, n_gz - 1),
            sems(2, n_gz - 1),
            sems(2, n_gz - 1),
            sems(SOLVES, 2),
            sems(SOLVES, 2),
            sems(n_gx - 1),
            sems(n_gx - 1),
        ],
        compiler_params=pltpu.CompilerParams(
            collective_id=0, has_side_effects=True, vmem_limit_bytes=32 * 1024 * 1024
        ),
    )(rhs_field, heights.T, vert_coef, balance, pool)
    return pressure, coarse


def solution(mesh):
    placed = (P("gz", None, "gx"), P("gx", None), P(), P("gx", None))
    return jax.shard_map(
        functools.partial(on_device, mesh.shape["gz"], mesh.shape["gx"]),
        mesh=mesh,
        in_specs=placed,
        out_specs=(P("gz", None, "gx"), P("gx", "gz")),
        check_vma=False,
    )
```

```python
import functools

import jax
import jax.numpy as jnp
from jax import lax
from jax.experimental import pallas as pl
from jax.experimental.pallas import tpu as pltpu
from jax.sharding import PartitionSpec as P

SWEEPS = 2
SOLVES = 2 * SWEEPS
UNROLL = 16
MESH = pl.DeviceIdType.MESH


def relax_kernel(
    n_gz,
    n_gx,
    rhs_ref,
    heights_ref,
    coef_ref,
    balance_ref,
    pool_ref,
    p_ref,
    out_ref,
    side_inv,
    low_inv,
    upper,
    low_spike,
    up_spike,
    local,
    delta,
    ends,
    spikes,
    reduced,
    firsts,
    lasts,
    edge_spikes,
    halo_out,
    halo_in,
    pooled,
    bundles,
    outgoing,
    arrived,
    ends_send,
    ends_recv,
    spikes_send,
    spikes_recv,
    halo_send,
    halo_recv,
    tail_send,
    tail_recv,
):
    levels, rows, width = rhs_ref.shape
    total_z = coef_ref.shape[0]
    gz = lax.axis_index("gz")
    gx = lax.axis_index("gx")
    first_level = gz * levels

    barrier = pltpu.get_barrier_semaphore()
    for o in range(1, n_gz):
        pl.semaphore_signal(
            barrier, inc=1, device_id=(gx, lax.rem(gz + o, n_gz)), device_id_type=MESH
        )
    for o in range(1, n_gx):
        pl.semaphore_signal(
            barrier, inc=1, device_id=(lax.rem(gx + o, n_gx), gz), device_id_type=MESH
        )

    zero = jnp.zeros((rows, width), jnp.float32)
    one = jnp.ones((rows, width), jnp.float32)
    lane = lax.broadcasted_iota(jnp.int32, (rows, width), 1)
    row = lax.broadcasted_iota(jnp.int32, (rows, width), 0)
    parity = lax.rem(lane + row + gx * width, 2)
    at_left = lane == 0
    at_right = lane == width - 1
    at_top = row == 0
    at_bottom = row == rows - 1

    @pl.when(gx == 0)
    def _():
        for t in range(SOLVES):
            halo_in[t, 0] = zero

    @pl.when(gx == n_gx - 1)
    def _():
        for t in range(SOLVES):
            halo_in[t, 1] = zero

    def fluid_at(k):
        return (first_level + k >= heights_ref[...]).astype(jnp.float32)

    def factor(k, carry):
        up_before, d_before, spike_before = carry
        z = first_level + k
        below = coef_ref[z]
        above = jnp.where(z + 1 < total_z, coef_ref[jnp.minimum(z + 1, total_z - 1)], 0.0)
        fluid = fluid_at(k)
        low = -below * fluid
        centre = fluid * (4.0 + below + above) + (1.0 - fluid)
        inverse = 1.0 / (centre - low * up_before)
        up = -above * fluid * inverse
        low = low * inverse
        scale = fluid * inverse
        d = rhs_ref[k] * scale - low * d_before
        spike = -low * spike_before
        upper[k] = up
        low_inv[k] = low
        side_inv[k] = scale
        local[k] = d
        low_spike[k] = spike
        return up, d, spike

    def turned(cells, shift):
        shift = shift % width
        return cells if shift == 0 else pltpu.roll(cells, shift, 1)

    def around(cells, edge, edge_mask):
        left = jnp.where(at_left, 0.0, pltpu.roll(cells, 1, 1))
        right = jnp.where(at_right, 0.0, pltpu.roll(cells, width - 1, 1))
        up = jnp.where(at_top, 0.0, pltpu.roll(cells, 1, 0))
        down = jnp.where(at_bottom, 0.0, pltpu.roll(cells, rows - 1, 0))
        return (left + right) + (up + down) + jnp.where(edge_mask, edge, 0.0)

    def forward(edge_mask, step, carry):
        d, edges = carry
        for j in range(UNROLL):
            k = step * UNROLL + j
            side = rhs_ref[k] + around(p_ref[k], turned(edges, -j), edge_mask)
            d = side * side_inv[k] - low_inv[k] * d
            local[k] = d
        return d, turned(edges, -UNROLL)

    def with_edge(packed, cells, i, offset):
        return jnp.where(lane == i + offset, turned(cells, i + 1), packed)

    def factor_back(step, carry):
        g, low, high, g_edge, low_right, low_left, high_right, high_left = carry
        base = levels - UNROLL * (step + 1)
        g_edge, low_right, low_left, high_right, high_left = (
            turned(edge, UNROLL)
            for edge in (g_edge, low_right, low_left, high_right, high_left)
        )
        for i in reversed(range(UNROLL)):
            k = base + i
            up = upper[k]
            g = local[k] - up * g
            low = low_spike[k] - up * low
            high = -up * high
            local[k] = g
            low_spike[k] = low
            up_spike[k] = high
            g_edge = with_edge(g_edge, g, i, edge_lane(0))
            low_right = with_edge(low_right, low, i, 0)
            low_left = with_edge(low_left, low, i, 1)
            high_right = with_edge(high_right, high, i, 0)
            high_left = with_edge(high_left, high, i, 1)
        return g, low, high, g_edge, low_right, low_left, high_right, high_left

    def backward(offset, step, carry):
        g, g_edge = carry
        base = levels - UNROLL * (step + 1)
        g_edge = turned(g_edge, UNROLL)
        for i in reversed(range(UNROLL)):
            k = base + i
            g = local[k] - upper[k] * g
            local[k] = g
            g_edge = with_edge(g_edge, g, i, offset)
        return g, g_edge

    def from_left(colour):
        return lax.rem(row + gx * width, 2) == colour

    def edge_lane(colour):
        return jnp.where(from_left(colour), 1, 0)

    def halo_copies(t):
        to_right = pltpu.make_async_remote_copy(
            src_ref=halo_out.at[t],
            dst_ref=halo_in.at[t, 0],
            send_sem=halo_send.at[t, 0],
            recv_sem=halo_recv.at[t, 0],
            device_id=(lax.rem(gx + 1, n_gx), gz),
            device_id_type=MESH,
        )
        to_left = pltpu.make_async_remote_copy(
            src_ref=halo_out.at[t],
            dst_ref=halo_in.at[t, 1],
            send_sem=halo_send.at[t, 1],
            recv_sem=halo_recv.at[t, 1],
            device_id=(lax.rem(gx + n_gx - 1, n_gx), gz),
            device_id_type=MESH,
        )
        return to_right, to_left

    def start_halo(t):
        to_right, to_left = halo_copies(t)

        @pl.when(gx < n_gx - 1)
        def _():
            to_right.start()

        @pl.when(gx > 0)
        def _():
            to_left.start()

    def finish_halo(t, colour):
        to_right, to_left = halo_copies(t)

        @pl.when(gx > 0)
        def _():
            to_left.wait_send()
            to_right.wait_recv()

        @pl.when(gx < n_gx - 1)
        def _():
            to_right.wait_send()
            to_left.wait_recv()

        left_edge = halo_in[t, 0]
        right_edge = turned(halo_in[t, 1], -2)
        return jnp.where(from_left(colour), left_edge, right_edge)

    def column_copy(ref, send, recv, o):
        return pltpu.make_async_remote_copy(
            src_ref=ref,
            dst_ref=ref,
            send_sem=send.at[o - 1],
            recv_sem=recv.at[o - 1],
            device_id=(gx, lax.rem(gz + o, n_gz)),
            device_id_type=MESH,
        )

    for t in range(SOLVES):
        colour = t % 2
        if t == 0:
            lax.fori_loop(0, levels, factor, (zero, zero, one), unroll=UNROLL)
            d_last = local[levels - 1]
            spikes[gz, 0] = low_spike[levels - 1]
            spikes[gz, 1] = -upper[levels - 1]
            pl.semaphore_wait(barrier, n_gz + n_gx - 2)
            early = [
                column_copy(
                    spikes.at[gz, pl.ds(0, 2)], spikes_send.at[0], spikes_recv.at[0], o
                )
                for o in range(1, n_gz)
            ]
            for copy in early:
                copy.start()
            g, low, high, g_edge, *spike_edges = lax.fori_loop(
                0, levels // UNROLL, factor_back, (zero, zero, one) + (zero,) * 5
            )
            spikes[gz, 2] = low
            spikes[gz, 3] = high
            for e in range(4):
                edge_spikes[e] = spike_edges[e]
        else:
            edge_mask = (at_left | at_right) & (parity == colour)
            d_last, _ = lax.fori_loop(
                0,
                levels // UNROLL,
                functools.partial(forward, edge_mask),
                (zero, finish_halo(t - 1, colour)),
            )
            g, g_edge = lax.fori_loop(
                0,
                levels // UNROLL,
                functools.partial(backward, edge_lane(colour)),
                (zero, zero),
            )
        ends[t, gz] = jnp.where(parity == colour, g, turned(d_last, 1))
        copies = [
            column_copy(ends.at[t, gz], ends_send.at[t], ends_recv.at[t], o)
            for o in range(1, n_gz)
        ]
        if t == 0:
            copies += [
                column_copy(
                    spikes.at[gz, pl.ds(2, 2)], spikes_send.at[1], spikes_recv.at[1], o
                )
                for o in range(1, n_gz)
            ]
        for copy in copies:
            copy.start()
        if t == 0:
            copies += early
        for copy in copies:
            copy.wait()

        if t == 0:
            beta = zero
            for s in range(n_gz):
                inverse = 1.0 / (1.0 - spikes[s, 2] * beta)
                reduced[s, 0] = beta
                reduced[s, 1] = inverse
                reduced[s, 2] = spikes[s, 3] * inverse
                beta = spikes[s, 1] + spikes[s, 0] * beta * reduced[s, 2]
                reduced[s, 3] = beta
        alpha = zero
        heads, tails = [], []
        for s in range(n_gz):
            both = ends[t, s]
            head = (both + spikes[s, 2] * alpha) * reduced[s, 1]
            alpha = turned(both, -1) + spikes[s, 0] * (alpha + reduced[s, 0] * head)
            heads.append(head)
            tails.append(alpha)
        after = zero
        firsts[n_gz] = zero
        lasts[0] = zero
        for s in reversed(range(n_gz)):
            lasts[s + 1] = tails[s] + reduced[s, 3] * after
            after = heads[s] + reduced[s, 2] * after
            firsts[s] = after
        below_value = lasts[gz]
        above_value = firsts[gz + 1]

        sent = from_left(colour)
        below_edge = jnp.where(sent, below_value[:, :1], below_value[:, width - 1 :])
        above_edge = jnp.where(sent, above_value[:, :1], above_value[:, width - 1 :])
        low_edge = jnp.where(sent, edge_spikes[1], edge_spikes[0])
        high_edge = jnp.where(sent, edge_spikes[3], edge_spikes[2])
        edge_cells = g_edge + low_edge * below_edge + high_edge * above_edge
        if t == SOLVES - 1:
            edge_cells = edge_cells - halo_out[t - 2]
        halo_out[t] = edge_cells
        start_halo(t)

        def correct(k, carry):
            value = local[k] + low_spike[k] * below_value + up_spike[k] * above_value
            before = zero if t == 0 else p_ref[k]
            cells = jnp.where(parity == colour, value, before)
            p_ref[k] = cells
            if t == SOLVES - 1:
                delta[k] = cells - before
            return carry

        lax.fori_loop(0, levels, correct, 0, unroll=UNROLL)

    edge_mask = (at_left | at_right) & (parity == 0)

    def coarsen(step, edges):
        for j in range(0, UNROLL, 2):
            k = step * UNROLL + j
            local[step * (UNROLL // 2) + j // 2] = fluid_at(k) * around(
                delta[k], turned(edges, -j), edge_mask
            ) + fluid_at(k + 1) * around(delta[k + 1], turned(edges, -j - 1), edge_mask)
        return turned(edges, -UNROLL)

    lax.fori_loop(0, levels // UNROLL, coarsen, finish_halo(SOLVES - 1, 0))

    half = rows // 2
    per_row = width // (width // 4)
    chunks = levels // 2 // per_row
    for i in range(levels // 2):
        c, part = i // per_row, i % per_row
        pooled[c * half : (c + 1) * half, part * width : (part + 1) * width] = (
            local[i, pl.ds(0, half, 2), :] + local[i, pl.ds(1, half, 2), :]
        )
    packed = jnp.dot(
        pooled[...],
        pool_ref[...],
        preferred_element_type=jnp.float32,
        precision=lax.Precision.HIGHEST,
    )
    for c in range(chunks):
        for h in range(2):
            bundles[h * half : (h + 1) * half, c, :] = packed[
                c * half : (c + 1) * half, h * width : (h + 1) * width
            ]
    share = rows // n_gx
    for j in range(rows):
        b = balance_ref[0, j]
        outgoing[j] = bundles[(b & 1) * half + (b >> 1)]
    copies = []
    for o in range(1, n_gx):
        owner = lax.rem(gx + o, n_gx)
        copies.append(
            pltpu.make_async_remote_copy(
                src_ref=outgoing.at[pl.ds(owner * share, share)],
                dst_ref=arrived.at[pl.ds(gx * share, share)],
                send_sem=tail_send.at[o - 1],
                recv_sem=tail_recv.at[o - 1],
                device_id=(owner, gz),
                device_id_type=MESH,
            )
        )
    for copy in copies:
        copy.start()
    arrived[pl.ds(gx * share, share)] = outgoing[pl.ds(gx * share, share)]
    for copy in copies:
        copy.wait()
    for c in range(chunks):
        out_ref[:, c * width : (c + 1) * width] = arrived[:, c, :]


def on_device(n_gz, n_gx, rhs_field, heights, vert_coef, balance):
    levels, rows, width = rhs_field.shape
    per_row = 4
    chunks = levels // 2 // per_row
    spot = jnp.arange(per_row * width, dtype=jnp.int32)[:, None]
    target = jnp.arange(2 * width, dtype=jnp.int32)[None, :]
    quarter = width // 4
    coarse_x = (spot % width) // 2
    pool = jnp.where(
        (target // width == coarse_x // quarter)
        & (target % width == (spot // width) * quarter + coarse_x % quarter),
        0.125,
        0.0,
    ).astype(jnp.float32)
    vmem = pl.BlockSpec(memory_space=pltpu.VMEM)
    smem = pl.BlockSpec(memory_space=pltpu.SMEM)
    slab = pltpu.VMEM((levels, rows, width), jnp.float32)
    plane = (rows, width)

    def planes(*lead):
        return pltpu.VMEM(lead + plane, jnp.float32)

    def sems(*lead):
        return pltpu.SemaphoreType.DMA(lead)

    pressure, coarse = pl.pallas_call(
        functools.partial(relax_kernel, n_gz, n_gx),
        out_shape=(
            jax.ShapeDtypeStruct(rhs_field.shape, jnp.float32),
            jax.ShapeDtypeStruct((rows, chunks * width), jnp.float32),
        ),
        in_specs=[vmem, vmem, smem, smem, vmem],
        out_specs=(vmem, vmem),
        scratch_shapes=[slab] * 7
        + [
            planes(SOLVES, n_gz),
            planes(n_gz, 4),
            planes(n_gz, 4),
            planes(n_gz + 1),
            planes(n_gz + 1),
            planes(4),
            planes(SOLVES),
            planes(SOLVES, 2),
            pltpu.VMEM((chunks * rows // 2, per_row * width), jnp.float32),
            pltpu.VMEM((rows, chunks, width), jnp.float32),
            pltpu.VMEM((rows, chunks, width), jnp.float32),
            pltpu.VMEM((rows, chunks, width), jnp.float32),
            sems(SOLVES, n_gz - 1),
            sems(SOLVES, n_gz - 1),
            sems(2, n_gz - 1),
            sems(2, n_gz - 1),
            sems(SOLVES, 2),
            sems(SOLVES, 2),
            sems(n_gx - 1),
            sems(n_gx - 1),
        ],
        compiler_params=pltpu.CompilerParams(
            collective_id=0, has_side_effects=True, vmem_limit_bytes=32 * 1024 * 1024
        ),
    )(rhs_field, heights.T, vert_coef, balance, pool)
    return pressure, coarse


def solution(mesh):
    placed = (P("gz", None, "gx"), P("gx", None), P(), P("gx", None))
    return jax.shard_map(
        functools.partial(on_device, mesh.shape["gz"], mesh.shape["gx"]),
        mesh=mesh,
        in_specs=placed,
        out_specs=(P("gz", None, "gx"), P("gx", "gz")),
        check_vma=False,
    )
```
